32 devices in a mesh: head: 4 (over y, x), blk: 8 (over z, core).
Axes of the slice: x: 2, y: 2, z: 4, core: 2. Of those that a mesh axis runs over, the one named last changes fastest.
Arguments:
- tokens: bfloat16 [2, 2048, 1792], P(None, ('head', 'blk')), may hold values from -6 to 6
- cotangent: bfloat16 [2, 2048, 1792], P(None, ('head', 'blk')), may hold values from -6 to 6
- teacher: bfloat16 [2, 2048, 1792], P(None, ('head', 'blk')), may hold values from -36 to 36
- lengths: int32 [2], replicated, may hold values from 512 to 2048, as said below
- gain_attn: float32 [1792], replicated, may hold values from 0.5 to 1.5
- gain_mlp: float32 [1792], replicated, may hold values from 0.5 to 1.5
- w_query: bfloat16 [1792, 256], P(('head', 'blk')), may hold values from -0.125 to 0.125
- w_key: bfloat16 [1792, 256], P(('head', 'blk')), may hold values from -0.125 to 0.125
- w_value: bfloat16 [1792, 1792], P(('head', 'blk')), may hold values from -0.125 to 0.125
- w_out: bfloat16 [1792, 1792], P(('head', 'blk')), may hold values from -2 to 2
- w_gate: bfloat16 [1792, 4864], P(('head', 'blk')), may hold values from -0.125 to 0.125
- w_up: bfloat16 [1792, 4864], P(('head', 'blk')), may hold values from -0.125 to 0.125
- w_down: bfloat16 [4864, 1792], P(('head', 'blk')), may hold values from -0.078125 to 0.078125
Outputs:
- out: bfloat16 [2, 2048, 1792], P(None, ('head', 'blk'))
- loss: float32 [], replicated
- grad_tokens: float32 [2, 2048, 1792], P(None, ('head', 'blk'))
- grad_w_query: float32 [1792, 256], P(('head', 'blk'))
- grad_w_key: float32 [1792, 256], P(('head', 'blk'))
- grad_w_value: float32 [1792, 1792], P(('head', 'blk'))
- grad_w_out: float32 [1792, 1792], P(('head', 'blk'))
- grad_w_gate: float32 [1792, 4864], P(('head', 'blk'))
- grad_w_up: float32 [1792, 4864], P(('head', 'blk'))
- grad_w_down: float32 [4864, 1792], P(('head', 'blk'))
- grad_gain_attn: float32 [1792], P(('head', 'blk'))
- grad_gain_mlp: float32 [1792], P(('head', 'blk'))
The draws below stay inside these ranges and needn't reach their ends.
Inputs may be any that keep to these rules, and one draw needn't show every extreme that they name: `lengths`: one sequence, which one varies, fills all 2048 slots; each has at least 512 valid slots.
All inputs are finite; a program needn't handle non-finite values.
Results may differ from the reference program's by a relative error of at most 0.015.
Values may be sent and summed in bfloat16 or wider, within the bound.
No kernel may reach another device: no remote copies, remote signals or barrier semaphores. Data moves between devices by JAX's collectives and lax.ppermute only.
A program may use at most 384 MiB of HBM per device.

```python
import math
import jax
import jax.numpy as jnp
import numpy as np
from jax import lax

D = 1792
H = 16
F = 16
FF = 4864
FE = 153
SEQS = 2
CAP = 2048


def draw_lengths(key, part):
    key = jax.random.fold_in(key, 11)
    first_key, second_key = jax.random.split(key)
    drawn_lengths = jax.random.randint(first_key, (SEQS,), CAP // 4, CAP + 1)
    longest = jax.random.randint(second_key, (), 0, SEQS)
    return jnp.where(jnp.arange(SEQS) == longest, CAP, drawn_lengths).astype(jnp.int32)


def draw_teacher(key, part):
    key = jax.random.fold_in(key, 23)
    first_key, second_key = jax.random.split(key, 2)
    position_ramp = 1.0 + 2.0 * jnp.arange(CAP, dtype=jnp.float32) / CAP
    seq_scale = jax.random.uniform(first_key, (SEQS, 1, 1), jnp.float32, 0.5, 2.0)
    base_values = jnp.clip(jax.random.normal(second_key, (SEQS, CAP, D), jnp.float32), -6.0, 6.0)
    return (base_values * seq_scale * position_ramp[None, :, None]).astype(jnp.bfloat16)


def level_of(stream_key, dims, cuts, smallest, largest):
    def one(axis_at, parts):
        draws = jax.random.uniform(jax.random.fold_in(jax.random.fold_in(stream_key, 6), axis_at), (parts,), jnp.float32, smallest / len(cuts), largest / len(cuts))
        return jnp.repeat(jnp.exp(draws), dims[axis_at] // parts).reshape((-1,) + (1,) * (len(dims) - axis_at - 1))

    loudness = one(*cuts[0])
    for cut in cuts[1:]:
        loudness = loudness * one(*cut)
    return loudness


def noise(own_key, dims, spread, most, cuts=(), held_as=jnp.bfloat16):
    entries = spread * jax.random.normal(own_key, dims, jnp.float32)
    if cuts:
        entries = entries * level_of(own_key, dims, cuts, -0.22, 0.18)
    return jnp.clip(entries, -most, most).astype(held_as)


def setup_inputs(seed: int = 0) -> dict:
    arg_keys = jax.random.split(jax.random.key(seed), 14)
    tokens = noise(arg_keys[0], (SEQS, CAP, D), 1.0, 6.0, ((1, 32),))
    cotangent = noise(arg_keys[1], (SEQS, CAP, D), 1.0, 6.0, ((1, 32),))
    teacher = draw_teacher(jax.random.fold_in(arg_keys[13], 71), 0)
    lengths = draw_lengths(jax.random.fold_in(arg_keys[13], 71), 0)
    gain_attn = jnp.clip(1.0 + 0.1 * jax.random.normal(arg_keys[4], (D,), jnp.float32), 0.5, 1.5)
    gain_mlp = jnp.clip(1.0 + 0.1 * jax.random.normal(arg_keys[5], (D,), jnp.float32), 0.5, 1.5)
    w_query = noise(arg_keys[6], (D, H * F), D ** -0.5, 0.125, ((0, 32),))
    w_key = noise(arg_keys[7], (D, H * F), D ** -0.5, 0.125, ((0, 32),))
    w_value = noise(arg_keys[8], (D, D), D ** -0.5, 0.125, ((0, 32),))
    w_out = noise(arg_keys[9], (D, D), (max(D // 256, 1)) ** -0.5, 2.0, ((0, 32),))
    w_gate = noise(arg_keys[10], (D, FF), D ** -0.5, 0.125, ((0, 32),))
    w_up = noise(arg_keys[11], (D, FF), D ** -0.5, 0.125, ((0, 32),))
    w_down = noise(arg_keys[12], (FF, D), FF ** -0.5, 0.078125, ((0, 32),))
    return {"tokens": tokens, "cotangent": cotangent, "teacher": teacher, "lengths": lengths, "gain_attn": gain_attn, "gain_mlp": gain_mlp, "w_query": w_query, "w_key": w_key, "w_value": w_value, "w_out": w_out, "w_gate": w_gate, "w_up": w_up, "w_down": w_down}


@jax.custom_vjp
def low(v):
    return lax.optimization_barrier(v.astype(jnp.bfloat16)).astype(jnp.float32)

@jax.custom_vjp
def low_back(v):
    return v

def low_keep(v):
    return (low(v), None)

def low_pass(kept, grad):
    return (grad,)

def back_keep(v):
    return (v, None)

def back_low(kept, grad):
    return (low(grad),)
low.defvjp(low_keep, low_pass)
low_back.defvjp(back_keep, back_low)
norm_eps = 1e-06
highest = lax.Precision.HIGHEST

def feature_map(vectors):
    feat_width = vectors.shape[-1]
    upper_row, upper_col = np.triu_indices(feat_width)
    weights = np.where(upper_row == upper_col, 1.0, math.sqrt(2.0)) / math.sqrt(2.0 * feat_width)
    ones_col = jnp.ones(vectors.shape[:-1] + (1,), jnp.float32)
    linear = vectors * feat_width ** (-0.25)
    square = vectors[..., upper_row] * vectors[..., upper_col] * jnp.asarray(weights, jnp.float32)
    return jnp.concatenate([ones_col, linear, square], axis=-1)

def dot_high(left_op, right_op):
    return jnp.dot(left_op, right_op, precision=highest)

def rms_scale(values):
    return lax.rsqrt(lax.optimization_barrier(jnp.mean(values * values, axis=-1, keepdims=True)) + norm_eps)

def attend(query_rows, key_rows, value_rows):
    slot_count = query_rows.shape[0]
    block_len = math.gcd(slot_count, 512)
    blocks_n = slot_count // block_len
    feat_query = low(feature_map(query_rows.reshape(slot_count, H, F)))
    feat_key = low(feature_map(key_rows.reshape(slot_count, H, F)))
    value_heads = value_rows.reshape(slot_count, H, D // H)
    causal_mask = jnp.tril(jnp.ones((block_len, block_len), jnp.float32))

    def block_step(carried, pieces):
        state_sum, key_sum = carried
        block_query, block_key, block_value = pieces
        scores = jnp.einsum('chf,dhf->hcd', block_query, block_key, precision=highest) * causal_mask
        numerator = jnp.einsum('hcd,dhe->che', scores, block_value, precision=highest)
        numerator = numerator + jnp.einsum('chf,hfe->che', block_query, state_sum, precision=highest)
        denominator = lax.optimization_barrier(jnp.sum(scores, axis=-1)).T + jnp.einsum('chf,hf->ch', block_query, key_sum, precision=highest)
        state_sum = state_sum + jnp.einsum('dhf,dhe->hfe', block_key, block_value, precision=highest)
        key_sum = key_sum + lax.optimization_barrier(jnp.sum(block_key, axis=0))
        return ((state_sum, key_sum), numerator / denominator[..., None])
    start_carry = (jnp.zeros((H, FE, D // H), jnp.float32), jnp.zeros((H, FE), jnp.float32))
    pieces = (feat_query.reshape(blocks_n, block_len, H, FE), feat_key.reshape(blocks_n, block_len, H, FE), value_heads.reshape(blocks_n, block_len, H, D // H))
    _, mixed = lax.scan(jax.checkpoint(block_step), start_carry, pieces)
    return mixed.reshape(slot_count, D)

def reference(tokens, cotangent, teacher, lengths, gain_attn, gain_mlp, w_query, w_key, w_value, w_out, w_gate, w_up, w_down):
    row_block = math.gcd(CAP, 4096)
    valid_rows = (jnp.arange(CAP, dtype=jnp.int32)[None, :] < lengths[:, None]).astype(jnp.float32)[..., None]
    valid_count = jnp.sum(lengths).astype(jnp.float32)
    target = teacher.astype(jnp.float32)

    def forward(tokens_f, gain_one, gain_two, query_w, key_w, value_w, out_w, gate_w, up_w, down_w):

        def mlp_rows(pieces):
            resid_rows, mask_rows, target_rows = pieces
            normed = low(resid_rows * rms_scale(resid_rows) * gain_two)
            gate_rows = low_back(dot_high(normed, gate_w))
            up_rows = low_back(dot_high(normed, up_w))
            hidden = low(jax.nn.silu(gate_rows) * up_rows)
            ffn_rows = low_back(dot_high(hidden, down_w))
            out_rows = mask_rows * (resid_rows + ffn_rows)
            diff_rows = out_rows - target_rows
            return (out_rows, jnp.sum(mask_rows * diff_rows * diff_rows))

        def one_sequence(pieces):
            seq_tokens, seq_mask, seq_target = pieces
            normed = low(seq_tokens * rms_scale(seq_tokens) * gain_one)
            query_rows = low_back(low(dot_high(normed, query_w)))
            key_rows = low_back(low(dot_high(normed, key_w)))
            value_rows = low_back(low(dot_high(normed, value_w)))
            mixed = low_back(low(attend(query_rows, key_rows, value_rows)))
            residual = seq_tokens + low_back(dot_high(mixed, out_w))
            blocks_n = CAP // row_block
            out_rows, losses = lax.map(jax.checkpoint(mlp_rows), (residual.reshape(blocks_n, row_block, D), seq_mask.reshape(blocks_n, row_block, 1), seq_target.reshape(blocks_n, row_block, D)))
            return (out_rows.reshape(CAP, D), jnp.sum(losses))
        all_out, losses = lax.map(one_sequence, (tokens_f, valid_rows, target))
        return (all_out, jnp.sum(losses) / (D * valid_count))
    (out_full, loss), pull_back = jax.vjp(forward, tokens.astype(jnp.float32), gain_attn, gain_mlp, w_query.astype(jnp.float32), w_key.astype(jnp.float32), w_value.astype(jnp.float32), w_out.astype(jnp.float32), w_gate.astype(jnp.float32), w_up.astype(jnp.float32), w_down.astype(jnp.float32))
    gradients = pull_back((cotangent.astype(jnp.float32), jnp.ones((), jnp.float32)))
    return (out_full.astype(jnp.bfloat16), loss, gradients[0], gradients[3], gradients[4], gradients[5], gradients[6], gradients[7], gradients[8], gradients[9], gradients[1], gradients[2])
```

```python
import functools

import jax
import jax.numpy as jnp
from jax import lax
from jax.experimental import pallas as pl
from jax.experimental.pallas import tpu as pltpu
from jax.sharding import Mesh
from jax.sharding import PartitionSpec as P

H = 16
norm_eps = 1e-06
bf16, f32 = jnp.bfloat16, jnp.float32


def dot(a, b, ca, cb):
    return lax.dot_general(a, b, (((ca,), (cb,)), ((), ())), preferred_element_type=f32)


def swap(x, axis, o):
    n = lax.axis_size(axis)
    return lax.ppermute(x, axis, [(i, i ^ o) for i in range(n)])


def rms_scale(values):
    return lax.rsqrt(jnp.mean(values * values, axis=-1, keepdims=True) + norm_eps)


BLK, CROSS = ("z", "c"), ("head", "c")


def tie(*values):
    return lax.optimization_barrier(values)


def spread(x, beside=()):
    got, beside = tie([swap(x, "head", o) for o in range(1, lax.axis_size("head"))], beside)
    return jnp.concatenate([x] + got, axis=1), beside


def collect(part, rows, beside=()):
    n = lax.axis_size("head")
    got = [swap(part[:, o * rows : (o + 1) * rows].astype(bf16), "head", o) for o in range(1, n)]
    got, beside = tie(got, beside)
    return sum([x.astype(f32) for x in got], part[:, :rows]), beside


def line_gather(x, beside=()):
    (near, far), beside = tie([swap(x, "z", 1), swap(x, "z", 2)], beside)
    return [x, near, far, swap(far, "z", 1)], beside


def line_sum(blocks, beside=()):
    by_way, beside = tie(swap(blocks[3], "z", 1), beside)
    far = (blocks[2].astype(f32) + by_way.astype(f32)).astype(bf16)
    return blocks[0].astype(f32) + swap(blocks[1], "z", 1).astype(f32) + swap(far, "z", 2).astype(f32), beside


def turn(pieces, axis):
    n, me = lax.axis_size(axis), lax.axis_index(axis)
    got = [pick(pieces, me)] + [swap(pick(pieces, me ^ o), axis, o) for o in range(1, n)]
    return in_place(got, me)


def turn_far(pieces):
    z = lax.axis_index("z")
    here = jnp.stack([pick(pieces, z), pick(pieces, z ^ 1)])
    there = jnp.stack([pick(pieces, z ^ 2), pick(pieces, z ^ 3)])
    return here, swap(there, "z", 2)


def turn_near(here, there):
    got = swap(jnp.stack([here[1], there[1]]), "z", 1)
    return in_place([here[0], got[0], there[0], got[1]], lax.axis_index("z"))


def line_sum_direct(blocks, beside=()):
    got, beside = tie([swap(blocks[o], "z", o) for o in range(1, 4)], beside)
    return sum([x.astype(f32) for x in got], blocks[0].astype(f32)), beside


def exchange(rel, beside=()):
    cores = lax.axis_size("c")
    halves = rel.reshape((4, cores) + rel.shape[1:])
    near = jnp.stack([halves[:, 0]] + [swap(halves[:, k], "c", k) for k in range(1, cores)], axis=1)
    got, beside = tie([swap(near[o], "z", o) for o in range(1, 4)], beside)
    return jnp.stack([near[0]] + got).reshape(rel.shape), beside


def in_place(got, me):
    whole = jnp.zeros((len(got),) + got[0].shape, got[0].dtype)
    for o, x in enumerate(got):
        whole = lax.dynamic_update_index_in_dim(whole, x, me ^ o, 0)
    return whole


def pick(x, i, axis=0):
    return lax.dynamic_index_in_dim(x, i, axis, keepdims=False)


def gather_blk(x, beside=()):
    got, beside = line_gather(x, beside)
    return gather_cores(got), beside


def gather_cores(got):
    got = in_place(got, lax.axis_index("z"))
    got = [got] + [swap(got, "c", k) for k in range(1, lax.axis_size("c"))]
    return jnp.moveaxis(in_place(got, lax.axis_index("c")), 0, 1)


def near_sum(parts, at):
    c = lax.axis_index("c")
    total = pick(parts, c, at).astype(f32)
    for k in range(1, lax.axis_size("c")):
        total = total + swap(pick(parts, c ^ k, at), "c", k).astype(f32)
    return total.astype(bf16)


def far_sum(near, at, beside=()):
    z = lax.axis_index("z")
    return line_sum([pick(near, z ^ o, at) for o in range(4)], beside)


def positions(b, sub, cps, slot, dim, sb):
    shape = (sb, 1) if dim == 0 else (1, sb)
    lane = lax.broadcasted_iota(jnp.int32, shape, dim)
    return ((b ^ (sub * cps + lane // slot)) * slot) + lane % slot


def flip(x):
    return jnp.transpose(x.astype(f32)).astype(bf16)


def kernel_sum(score):
    lifted = score + 4.0
    return lifted * lifted * (1.0 / 32.0) + 0.5


def fwd_kernel(nh, nb, slot, sb, ids, got, tiles, res, out, vrow):
    nsub, cps = nb * slot // sb, sb // slot
    h, b = ids[0], ids[1]
    for o in range(nb):
        for oh in range(nh):
            at = (h ^ oh) * nsub + o // cps
            lo = (o % cps) * slot
            tiles[at, :, lo : lo + slot] = got[o, :, oh * slot : (oh + 1) * slot]

    def rows_of(i, c):
        vv = jnp.concatenate([tiles[i, 32:144, :].astype(f32), jnp.ones((16, sb), f32)], axis=0)
        vrow[i] = jnp.transpose(vv).astype(bf16)
        return c

    lax.fori_loop(0, nh * nsub, rows_of, 0)

    for oh in range(nh):
        hq = h ^ oh
        for sub in range(nsub):
            iq = hq * nsub + sub
            qrow = flip(tiles[iq, 0:16, :])
            pos_q = positions(b, sub, cps, slot, 0, sb)

            def step(ik, acc, masked):
                w = kernel_sum(dot(qrow, tiles[ik, 16:32, :], 1, 0))
                if masked:
                    pos_k = positions(b, ik - hq * nsub, cps, slot, 1, sb)
                    w = jnp.where(pos_q >= pos_k, w, 0.0)
                return acc + dot(w.astype(bf16), vrow[ik], 1, 0)

            acc = lax.fori_loop(
                0, hq * nsub, functools.partial(step, masked=False), jnp.zeros((sb, 128), f32)
            )
            acc = lax.fori_loop(hq * nsub, (hq + 1) * nsub, functools.partial(step, masked=True), acc)
            den = acc[:, 112:113]
            mixed = acc / den
            lane = lax.broadcasted_iota(jnp.int32, (sb, 128), 1)
            res[iq] = jnp.where(lane == 112, den, mixed)
            back = jnp.transpose(mixed)[0:112].astype(bf16)
            for c in range(cps):
                out[sub * cps + c, :, oh * slot : (oh + 1) * slot] = back[:, c * slot : (c + 1) * slot]


def bwd_kernel(nh, nb, slot, sb, ids, tiles, res, got, out, gt, krow, acc):
    nsub, cps = nb * slot // sb, sb // slot
    h, b = ids[0], ids[1]
    for o in range(nb):
        for oh in range(nh):
            at = (h ^ oh) * nsub + o // cps
            lo = (o % cps) * slot
            gt[at, :, lo : lo + slot] = got[o, :, oh * slot : (oh + 1) * slot]

    def rows_of(i, c):
        krow[i] = flip(tiles[i, 16:32, :])
        acc[i] = jnp.zeros((144, sb), f32)
        return c

    lax.fori_loop(0, nh * nsub, rows_of, 0)

    for oh in range(nh):
        hq = h ^ oh
        for sub in range(nsub):
            iq = hq * nsub + sub
            qcol = tiles[iq, 0:16, :]
            qrow = flip(qcol)
            gcol = gt[iq]
            grow = jnp.transpose(gcol.astype(f32))
            kept = res[iq]
            rden = 1.0 / kept[:, 112:113]
            delta = jnp.sum(grow * kept[:, 0:112], axis=1, keepdims=True)
            grow = grow.astype(bf16)
            pos_q = positions(b, sub, cps, slot, 0, sb)

            def step(ik, dq, masked):
                lifted = dot(qrow, tiles[ik, 16:32, :], 1, 0) + 4.0
                g = (dot(grow, tiles[ik, 32:144, :], 1, 0) - delta) * rden
                p = (lifted * lifted * (1.0 / 32.0) + 0.5) * rden
                ds = g * lifted * (1.0 / 16.0)
                if masked:
                    pos_k = positions(b, ik - hq * nsub, cps, slot, 1, sb)
                    keep = pos_q >= pos_k
                    p = jnp.where(keep, p, 0.0)
                    ds = jnp.where(keep, ds, 0.0)
                p, ds = p.astype(bf16), ds.astype(bf16)
                acc[ik, 32:144, :] += dot(gcol, p, 1, 0)
                acc[ik, 16:32, :] += dot(qcol, ds, 1, 0)
                return dq + dot(ds, krow[ik], 1, 0)

            dq = lax.fori_loop(
                0, hq * nsub, functools.partial(step, masked=False), jnp.zeros((sb, 16), f32)
            )
            dq = lax.fori_loop(hq * nsub, (hq + 1) * nsub, functools.partial(step, masked=True), dq)
            acc[iq, 0:16, :] = jnp.transpose(dq)
    for oh in range(nh):
        for o in range(nb):
            at = (h ^ oh) * nsub + o // cps
            lo = (o % cps) * slot
            out[o, :, oh * slot : (oh + 1) * slot] = acc[at, :, lo : lo + slot].astype(bf16)


def call(body, ids, arrays, outs, scratch):
    vmem = pl.BlockSpec(memory_space=pltpu.VMEM)
    return pl.pallas_call(
        body,
        out_shape=outs,
        in_specs=[pl.BlockSpec(memory_space=pltpu.SMEM)] + [vmem] * len(arrays),
        out_specs=jax.tree.map(lambda _: vmem, outs),
        scratch_shapes=scratch,
        compiler_params=pltpu.CompilerParams(vmem_limit_bytes=48 * 1024 * 1024),
    )(ids, *arrays)


def shards(
    tokens,
    cotangent,
    teacher,
    lengths,
    gain_attn,
    gain_mlp,
    w_query,
    w_key,
    w_value,
    w_out,
    w_gate,
    w_up,
    w_down,
):
    seqs, slot, width = tokens.shape
    cores = lax.axis_size("c")
    nh, nb = lax.axis_size("head"), 4 * cores
    h, b = lax.axis_index("head"), lax.axis_index(BLK)
    hd = H // nh
    pairs = seqs * hd
    copies = nb // pairs
    drow = w_query.shape[0]
    fw, vw = w_query.shape[1] // H, w_value.shape[1] // H
    pw = 2 * fw + vw
    ffl = w_gate.shape[1] // 4
    lanes = nh * slot
    sb = min(512, nb * slot)
    n = nb * slot * nh // sb
    ids = jnp.stack([h, b]).astype(jnp.int32)

    def columns(ws):
        return jnp.concatenate([w.reshape(drow, nh, -1).transpose(1, 0, 2) for w in ws], axis=2)

    def line_columns(ws):
        ws = [w.reshape(drow, nh, 4, -1).transpose(2, 0, 1, 3).reshape(4, drow, -1) for w in ws]
        return jnp.concatenate(ws, axis=2)

    def gathered(x):
        return lax.all_gather(x[None], CROSS, axis=0, tiled=True)

    down_w = gathered(w_down).reshape(-1, width)
    qkv_cols = turn(columns((w_query, w_key, w_value)), "head")
    qkv_line, (tokens, w_gate_late, w_up_late) = line_gather(qkv_cols, (tokens, w_gate, w_up))
    ffn_cols = turn_far(line_columns((w_gate_late, w_up_late)))

    place = (h * nb + b) * slot + lax.broadcasted_iota(jnp.int32, (seqs, slot), 1)
    valid = (place < lengths[:, None]).astype(f32)[..., None]
    count = jnp.sum(lengths).astype(f32)

    tokens_f = tokens.astype(f32)
    scale_one = rms_scale(tokens_f)
    qkv_w = gather_cores(qkv_line)
    qkv_w = qkv_w.transpose(2, 0, 1, 3, 4).reshape(width, -1)
    normed_attn, ffn_cols = spread((tokens_f * scale_one * gain_attn).astype(bf16), ffn_cols)
    normed_attn = normed_attn.reshape(-1, width)
    ffn_w = gathered(turn_near(*ffn_cols))
    ffn_w = ffn_w.reshape(nh, cores, 4, drow, -1).transpose(0, 2, 1, 3, 4).reshape(width, -1)
    qkv = dot(qkv_w, normed_attn, 0, 1).astype(bf16)

    def to_pairs(rows, sizes):
        parts, at = [], 0
        for size in sizes:
            parts.append(rows[at : at + hd * size].reshape(hd, size, seqs, lanes))
            at += hd * size
        return jnp.concatenate(parts, axis=1).transpose(2, 0, 1, 3).reshape(pairs, -1, lanes)

    def send_pairs(pieces, beside=()):
        return exchange(jnp.take(pieces, (b ^ jnp.arange(nb)) // copies, axis=0), beside)

    def back_pairs(pieces, sizes, beside=()):
        got, beside = exchange(pieces, beside)
        got = jnp.take(got, b ^ (jnp.arange(pairs) * copies), axis=0)
        got = got.reshape(seqs, hd, -1, lanes).transpose(1, 2, 0, 3)
        parts, at = [], 0
        for size in sizes:
            parts.append(got[:, at : at + size].reshape(hd * size, seqs * lanes))
            at += size
        return jnp.concatenate(parts, axis=0), beside

    geometry = (nh, nb, slot, sb)
    sent, (w_out_late, down_w) = send_pairs(to_pairs(qkv, (fw, fw, vw)), (w_out, down_w))
    out_w = gather_blk(w_out_late)[0].reshape(-1, width)
    tiles, res, mixed_out = call(
        functools.partial(fwd_kernel, *geometry),
        ids,
        [sent],
        [
            jax.ShapeDtypeStruct((n, pw, sb), bf16),
            jax.ShapeDtypeStruct((n, sb, 128), f32),
            jax.ShapeDtypeStruct((nb, vw, lanes), bf16),
        ],
        [pltpu.VMEM((n, sb, 128), bf16)],
    )
    mixed = back_pairs(mixed_out, (vw,))[0]
    attn_part = dot(mixed, out_w, 0, 0).reshape(seqs, lanes, width)
    attn_sum, (ffn_w,) = collect(attn_part, slot, (ffn_w,))
    residual = tokens_f + attn_sum

    scale_two = rms_scale(residual)
    normed_mlp, _ = line_gather((residual * scale_two * gain_mlp).astype(bf16))
    normed_mlp = [x.reshape(-1, width) for x in normed_mlp]
    gates, ups, hiddens, parts = [], [], [], []
    for x in normed_mlp:
        both = dot(x, ffn_w, 1, 0)
        gates.append(both[:, :ffl])
        ups.append(both[:, ffl:])
        hiddens.append((jax.nn.silu(gates[-1]) * ups[-1]).astype(bf16))
        parts.append(dot(hiddens[-1], down_w, 1, 0).reshape(seqs, slot, width))
    ffn_sum, _ = line_sum_direct([parts[0]] + [x.astype(bf16) for x in parts[1:]])
    full = valid * (residual + ffn_sum)
    diff = full - teacher.astype(f32)
    loss = jnp.sum(valid * diff * diff).reshape(1, 1)

    grad_res = valid * (cotangent.astype(f32) + 2.0 * valid * diff / (width * count))
    grad_ffn, (loss,) = line_gather(grad_res.astype(bf16), (loss + swap(loss, "head", 1),))
    grad_ffn = [x.reshape(-1, width) for x in grad_ffn]
    grad_boths, parts = [], []
    for x, gate, up in zip(grad_ffn, gates, ups):
        grad_hidden = dot(x, down_w, 1, 1)
        sigma = jax.nn.sigmoid(gate)
        slope = sigma * (1.0 + gate * (1.0 - sigma))
        grad_boths.append(
            jnp.concatenate(
                [(grad_hidden * up * slope).astype(bf16), (grad_hidden * gate * sigma).astype(bf16)],
                axis=1,
            )
        )
        parts.append(dot(grad_boths[-1], ffn_w, 1, 1).reshape(seqs, slot, width))
    parts = [parts[0]] + [x.astype(bf16) for x in parts[1:]]

    def norm_back(grad_norm, values, scale_rows, gain):
        unit = values * scale_rows
        e = grad_norm * gain
        return scale_rows * (e - unit * jnp.mean(e * unit, axis=-1, keepdims=True))

    parts, normed_mlp, grad_boths = tie(parts, normed_mlp, grad_boths)
    normed_mlp, grad_both = jnp.concatenate(normed_mlp), jnp.concatenate(grad_boths)
    hidden, grad_ffn = jnp.concatenate(hiddens), jnp.concatenate(grad_ffn)
    grad_ffn_w = dot(normed_mlp, grad_both, 0, 0).astype(bf16)
    grad_ffn_w = grad_ffn_w.reshape(nh, 4, cores, drow, -1).transpose(0, 2, 1, 3, 4)
    grad_ffn_w = grad_ffn_w.reshape(nb, 4 * drow, -1)
    grad_mid, (grad_ffn_w, hidden, loss) = line_sum(
        parts, (grad_ffn_w, hidden, loss + swap(loss, "head", 2))
    )
    grad_ffn_w = lax.psum_scatter(grad_ffn_w, CROSS, scatter_dimension=0)
    grad_down = dot(hidden, grad_ffn, 0, 0).astype(bf16).reshape(nb, -1, width)
    o = 1
    while o < cores:
        loss = loss + swap(loss, "c", o)
        o *= 2
    grad_mid, grad_down = tie(grad_mid, grad_down)
    grad_resid = grad_res + norm_back(grad_mid, residual, scale_two, gain_mlp)
    grad_attn, (loss,) = spread(grad_resid.astype(bf16), (loss + swap(loss, "z", 1),))
    grad_attn = grad_attn.reshape(-1, width)
    grad_mixed = dot(out_w, grad_attn, 1, 1).astype(bf16)
    grad_out_w = dot(mixed, grad_attn, 1, 0).astype(bf16).reshape(4, cores, drow, width)
    sent, (grad_out_w, grad_ffn_w, grad_down) = send_pairs(
        to_pairs(grad_mixed, (vw,)), (grad_out_w, grad_ffn_w, grad_down)
    )
    grad_ffn_w = turn_far(grad_ffn_w.reshape(4, drow, -1))
    grad_down = lax.psum_scatter(grad_down, CROSS, scatter_dimension=0)
    grad_out_w = near_sum(grad_out_w, 1)
    grads_out = call(
        functools.partial(bwd_kernel, *geometry),
        ids,
        [tiles, res, sent],
        jax.ShapeDtypeStruct((nb, pw, lanes), bf16),
        [
            pltpu.VMEM((n, vw, sb), bf16),
            pltpu.VMEM((n, sb, fw), bf16),
            pltpu.VMEM((n, pw, sb), f32),
        ],
    )
    grads_out, loss = tie(grads_out, loss + swap(loss, "z", 2))
    grad_qkv, (grad_ffn_w, grad_out_w) = back_pairs(
        grads_out, (fw, fw, vw), (grad_ffn_w, grad_out_w)
    )
    grad_qkv_w = dot(normed_attn, grad_qkv, 0, 1).astype(bf16).reshape(nh, 4, cores, drow, -1)
    attn_back = dot(grad_qkv, qkv_w, 0, 1).reshape(seqs, lanes, width)
    grad_qkv_w, attn_back = tie(near_sum(grad_qkv_w, 2), attn_back)
    grad_qkv_w, (grad_out_w, grad_ffn_w, grad_down) = far_sum(
        grad_qkv_w, 1, (grad_out_w, grad_ffn_w, grad_down)
    )
    grad_in, (grad_qkv_w, grad_out_w, grad_ffn_w) = collect(
        attn_back, slot, (grad_qkv_w, grad_out_w, grad_ffn_w)
    )
    grad_qkv_w = turn(grad_qkv_w.astype(bf16), "head")
    grad_ffn_w = turn_near(*grad_ffn_w)
    grad_out_w, _ = far_sum(grad_out_w, 0)
    grad_tokens = grad_resid + norm_back(grad_in, tokens_f, scale_one, gain_attn)
    loss = loss[0, 0] / (width * count)

    def whole(got, lo, hi):
        return got[:, :, lo:hi].transpose(1, 0, 2).reshape(drow, -1).astype(f32)

    def line_whole(got, lo, hi):
        got = got[:, :, lo:hi].reshape(4, drow, nh, -1).transpose(1, 2, 0, 3)
        return got.reshape(drow, -1).astype(f32)

    qw, vv = hd * fw, hd * vw
    gq, gk = whole(grad_qkv_w, 0, qw), whole(grad_qkv_w, qw, 2 * qw)
    gv = whole(grad_qkv_w, 2 * qw, 2 * qw + vv)
    gg, gu = line_whole(grad_ffn_w, 0, ffl), line_whole(grad_ffn_w, ffl, 2 * ffl)

    def gain_grad(pairs_of, gain):
        total = sum(jnp.sum(w.astype(f32) * g, axis=1) for w, g in pairs_of)
        return total / lax.dynamic_slice(gain, ((h * nb + b) * drow,), (drow,))

    return (
        full.astype(bf16),
        loss,
        grad_tokens,
        gq,
        gk,
        gv,
        grad_out_w.astype(f32),
        gg,
        gu,
        grad_down.astype(f32),
        gain_grad(((w_query, gq), (w_key, gk), (w_value, gv)), gain_attn),
        gain_grad(((w_gate, gg), (w_up, gu)), gain_mlp),
    )


def solution(mesh):
    parts = Mesh(mesh.devices.reshape(mesh.shape["head"], 4, -1), ("head",) + BLK)
    rows, slots = P(("head",) + BLK, None), P(None, ("head",) + BLK, None)
    return jax.shard_map(
        shards,
        mesh=parts,
        in_specs=(slots,) * 3 + (P(),) * 3 + (rows,) * 7,
        out_specs=(slots, P(), slots) + (rows,) * 7 + (P(("head",) + BLK),) * 2,
        check_vma=False,
    )
```

```python
import functools
import math

import jax
import jax.numpy as jnp
from jax import lax
from jax.experimental import pallas as pl
from jax.experimental.pallas import tpu as pltpu
from jax.sharding import Mesh
from jax.sharding import PartitionSpec as P

H = 16
norm_eps = 1e-06
bf16, f32 = jnp.bfloat16, jnp.float32


def dot(a, b, ca, cb):
    return lax.dot_general(a, b, (((ca,), (cb,)), ((), ())), preferred_element_type=f32)


def swap(x, axis, o):
    n = lax.axis_size(axis)
    return lax.ppermute(x, axis, [(i, i ^ o) for i in range(n)])


def rms_scale(values):
    return lax.rsqrt(jnp.mean(values * values, axis=-1, keepdims=True) + norm_eps)


HEAD, LINE, BLK, CROSS = "head", "z", ("z", "c"), ("head", "c")
AXES = (HEAD,) + BLK


def tie(*values):
    return lax.optimization_barrier(values)


def window(moves, beside=()):
    arrays = tie(*[x for x, _, _ in moves])
    return tie([swap(x, axis, o) for x, (_, axis, o) in zip(arrays, moves)], beside)


def over(x, axis):
    return [(x, axis, o) for o in range(1, lax.axis_size(axis))]


def turn_moves(pieces, axis):
    me = lax.axis_index(axis)
    return [(pick(pieces, me ^ o), axis, o) for o in range(1, lax.axis_size(axis))]


def turned(pieces, got, axis):
    me = lax.axis_index(axis)
    return in_place([pick(pieces, me)] + list(got), me)


def return_moves(parts, axis):
    return [(x, axis, o) for o, x in enumerate(parts) if o]


def plus(own, got):
    return sum([x.astype(f32) for x in got], own.astype(f32))


def by_way(blocks):
    return (blocks[3], LINE, 1)


def rest_moves(blocks, passing):
    far = (blocks[2].astype(f32) + passing.astype(f32)).astype(bf16)
    return [(blocks[1], LINE, 1), (far, LINE, 2)]


def exchange(pieces, far_moves=(), far_beside=()):
    got, _ = window([(pieces[k], "c", k) for k in range(1, pieces.shape[0])])
    near = jnp.stack([pieces[0]] + got, axis=1)
    got, far_beside = window([(near[o], LINE, o) for o in range(1, 4)] + list(far_moves), far_beside)
    return [near[0]] + got[:3], got[3:], far_beside


def in_place(got, me):
    whole = jnp.zeros((len(got),) + got[0].shape, got[0].dtype)
    for o, x in enumerate(got):
        whole = lax.dynamic_update_index_in_dim(whole, x, me ^ o, 0)
    return whole


def pick(x, i, axis=0):
    return lax.dynamic_index_in_dim(x, i, axis, keepdims=False)


def line_whole(got):
    return in_place(got, lax.axis_index(LINE))


def core_end(own, got):
    return jnp.moveaxis(in_place([own] + list(got), lax.axis_index("c")), 0, 1)


def core_share(parts, at):
    me = lax.axis_index("c")
    return [(pick(parts, me ^ o, at), "c", o) for o in range(1, lax.axis_size("c"))]


def core_sum(parts, got, at):
    return plus(pick(parts, lax.axis_index("c"), at), got).astype(bf16)


def line_blocks(near, at):
    return [pick(near, lax.axis_index(LINE) ^ o, at) for o in range(4)]


def positions(b, sub, cps, slot, dim, sb):
    shape = (sb, 1) if dim == 0 else (1, sb)
    lane = lax.broadcasted_iota(jnp.int32, shape, dim)
    return ((b ^ (sub * cps + lane // slot)) * slot) + lane % slot


def flip(x):
    return jnp.transpose(x.astype(f32)).astype(bf16)


def kernel_sum(score):
    lifted = score + 4.0
    return lifted * lifted * (1.0 / 32.0) + 0.5


def fwd_kernel(nh, nb, slot, sb, ids, got0, got1, got2, got3, tiles, res, out, vrow):
    got, cores = (got0, got1, got2, got3), nb // 4
    nsub, cps = nb * slot // sb, sb // slot
    h, b = ids[0], ids[1]
    for o in range(nb):
        for oh in range(nh):
            at = (h ^ oh) * nsub + o // cps
            lo = (o % cps) * slot
            piece = got[o // cores][o % cores, :, oh * slot : (oh + 1) * slot]
            tiles[at, :, lo : lo + slot] = piece

    def rows_of(i, c):
        vv = jnp.concatenate([tiles[i, 32:144, :].astype(f32), jnp.ones((16, sb), f32)], axis=0)
        vrow[i] = jnp.transpose(vv).astype(bf16)
        return c

    lax.fori_loop(0, nh * nsub, rows_of, 0)

    for oh in range(nh):
        hq = h ^ oh
        for sub in range(nsub):
            iq = hq * nsub + sub
            qrow = flip(tiles[iq, 0:16, :])
            pos_q = positions(b, sub, cps, slot, 0, sb)

            def step(ik, acc, masked):
                w = kernel_sum(dot(qrow, tiles[ik, 16:32, :], 1, 0))
                if masked:
                    pos_k = positions(b, ik - hq * nsub, cps, slot, 1, sb)
                    w = jnp.where(pos_q >= pos_k, w, 0.0)
                return acc + dot(w.astype(bf16), vrow[ik], 1, 0)

            acc = lax.fori_loop(
                0, hq * nsub, functools.partial(step, masked=False), jnp.zeros((sb, 128), f32)
            )
            acc = lax.fori_loop(hq * nsub, (hq + 1) * nsub, functools.partial(step, masked=True), acc)
            den = acc[:, 112:113]
            mixed = acc / den
            lane = lax.broadcasted_iota(jnp.int32, (sb, 128), 1)
            res[iq] = jnp.where(lane == 112, den, mixed)
            back = jnp.transpose(mixed)[0:112].astype(bf16)
            for c in range(cps):
                o = sub * cps + c
                piece = back[:, c * slot : (c + 1) * slot]
                out[o % cores, o // cores, :, oh * slot : (oh + 1) * slot] = piece


def bwd_kernel(nh, nb, slot, sb, ids, tiles, res, got0, got1, got2, got3, out, gt, krow, acc):
    got, cores = (got0, got1, got2, got3), nb // 4
    nsub, cps = nb * slot // sb, sb // slot
    h, b = ids[0], ids[1]
    for o in range(nb):
        for oh in range(nh):
            at = (h ^ oh) * nsub + o // cps
            lo = (o % cps) * slot
            piece = got[o // cores][o % cores, :, oh * slot : (oh + 1) * slot]
            gt[at, :, lo : lo + slot] = piece

    def rows_of(i, c):
        krow[i] = flip(tiles[i, 16:32, :])
        acc[i] = jnp.zeros((144, sb), f32)
        return c

    lax.fori_loop(0, nh * nsub, rows_of, 0)

    for oh in range(nh):
        hq = h ^ oh
        for sub in range(nsub):
            iq = hq * nsub + sub
            qcol = tiles[iq, 0:16, :]
            qrow = flip(qcol)
            gcol = gt[iq]
            grow = jnp.transpose(gcol.astype(f32))
            kept = res[iq]
            rden = 1.0 / kept[:, 112:113]
            delta = jnp.sum(grow * kept[:, 0:112], axis=1, keepdims=True)
            grow = grow.astype(bf16)
            pos_q = positions(b, sub, cps, slot, 0, sb)

            def step(ik, dq, masked):
                lifted = dot(qrow, tiles[ik, 16:32, :], 1, 0) + 4.0
                g = (dot(grow, tiles[ik, 32:144, :], 1, 0) - delta) * rden
                p = (lifted * lifted * (1.0 / 32.0) + 0.5) * rden
                ds = g * lifted * (1.0 / 16.0)
                if masked:
                    pos_k = positions(b, ik - hq * nsub, cps, slot, 1, sb)
                    keep = pos_q >= pos_k
                    p = jnp.where(keep, p, 0.0)
                    ds = jnp.where(keep, ds, 0.0)
                p, ds = p.astype(bf16), ds.astype(bf16)
                acc[ik, 32:144, :] += dot(gcol, p, 1, 0)
                acc[ik, 16:32, :] += dot(qcol, ds, 1, 0)
                return dq + dot(ds, krow[ik], 1, 0)

            dq = lax.fori_loop(
                0, hq * nsub, functools.partial(step, masked=False), jnp.zeros((sb, 16), f32)
            )
            dq = lax.fori_loop(hq * nsub, (hq + 1) * nsub, functools.partial(step, masked=True), dq)
            acc[iq, 0:16, :] = jnp.transpose(dq)
    for oh in range(nh):
        for o in range(nb):
            at = (h ^ oh) * nsub + o // cps
            lo = (o % cps) * slot
            piece = acc[at, :, lo : lo + slot].astype(bf16)
            out[o % cores, o // cores, :, oh * slot : (oh + 1) * slot] = piece


def rows_of(refs, s):
    return jnp.concatenate([x[s] for x in refs], axis=0)


def to_peers(cores, copies, b, pieces, out):
    for o in range(4 * cores):
        out[o % cores, o // cores] = pieces[(b ^ o) // copies]


def from_peers(cores, copies, b, got, pieces):
    for o in range(4 * cores):
        pieces[o] = got[o // cores][o % cores]
    return lambda p: pieces[b ^ (p * copies)]


def qkv_kernel(hd, copies, fw, vw, ids, x0, x1, x2, x3, w, out, pieces):
    cores = out.shape[0]
    for s in range(x0.shape[0]):
        rows = jnp.dot(rows_of((x0, x1, x2, x3), s), w[...], preferred_element_type=f32)
        cols = jnp.transpose(rows)
        for j in range(hd):
            at = (j * fw, (hd + j) * fw, 2 * hd * fw + j * vw)
            piece = [cols[lo : lo + n] for lo, n in zip(at, (fw, fw, vw))]
            pieces[s * hd + j] = jnp.concatenate(piece, axis=0).astype(bf16)
    to_peers(cores, copies, ids[1], pieces, out)


def out_kernel(hd, copies, ids, g0, g1, g2, g3, w, mixed, own, send, pieces):
    cores, vw, lanes = g0.shape
    seqs, slot = own.shape[:2]
    take = from_peers(cores, copies, ids[1], (g0, g1, g2, g3), pieces)
    for s in range(seqs):
        cols = jnp.concatenate([take(s * hd + j) for j in range(hd)], axis=0)
        mixed[:, s * lanes : (s + 1) * lanes] = cols
        rows = jnp.transpose(cols.astype(f32)).astype(bf16)
        part = jnp.dot(rows, w[...], preferred_element_type=f32)
        own[s] = part[:slot]
        for o in range(1, 4):
            send[o - 1, s] = part[o * slot : (o + 1) * slot].astype(bf16)


def mixed_back_kernel(hd, copies, ids, x0, x1, x2, x3, w, mixed, out, grad, pieces):
    cores, vw, lanes = out.shape[0], out.shape[2], out.shape[3]
    z, c = ids[2], ids[1] % cores
    rows = [rows_of((x0, x1, x2, x3), s) for s in range(x0.shape[0])]
    for s, x in enumerate(rows):
        cols = dot(w[...], x, 1, 1)
        for j in range(hd):
            pieces[s * hd + j] = cols[j * vw : (j + 1) * vw].astype(bf16)
    to_peers(cores, copies, ids[1], pieces, out)
    total = jnp.dot(mixed[...], jnp.concatenate(rows, axis=0), preferred_element_type=f32)
    drow = grad.shape[2]
    for k in range(4 * cores):
        grad[(k % cores) ^ c, (k // cores) ^ z] = total[k * drow : (k + 1) * drow].astype(bf16)


def qkv_back_kernel(hd, copies, fw, vw, ids, g0, g1, g2, g3, x, w, grad, own, send, pieces, cols):
    cores, pw, lanes = g0.shape
    seqs, slot = own.shape[:2]
    z, c = ids[2], ids[1] % cores
    take = from_peers(cores, copies, ids[1], (g0, g1, g2, g3), pieces)
    for s in range(seqs):
        for j in range(hd):
            piece = take(s * hd + j)
            at = (j * fw, (hd + j) * fw, 2 * hd * fw + j * vw)
            lo = 0
            for row, n in zip(at, (fw, fw, vw)):
                cols[row : row + n, s * lanes : (s + 1) * lanes] = piece[lo : lo + n]
                lo += n
    rows = jnp.transpose(cols[...].astype(f32)).astype(bf16)
    for s in range(seqs):
        part = dot(rows[s * lanes : (s + 1) * lanes], w[...], 1, 1)
        own[s] = part[:slot]
        for o in range(1, 4):
            send[o - 1, s] = part[o * slot : (o + 1) * slot].astype(bf16)
    drow, half = grad.shape[3], x.shape[1] // 2
    for i in range(2):
        total = dot(x[:, i * half : (i + 1) * half], rows, 0, 0)
        for k in range(half // drow):
            at = i * (half // drow) + k
            block = total[k * drow : (k + 1) * drow].astype(bf16)
            grad[(at % cores) ^ c, (at // cores % 4) ^ z, at // (4 * cores)] = block


def cut_kernel(nh, run, ids, gate, up, out):
    z = ids[2]
    for zz in range(4):
        parts = []
        for w in (gate, up):
            parts += [w[:, (k * 4 + zz) * run : (k * 4 + zz + 1) * run] for k in range(nh)]
        out[zz ^ z] = jnp.concatenate([x.astype(f32) for x in parts], axis=1).astype(bf16)


def feed_kernel(nh, run, ids, p0, p1, p2, p3, gate, up, grad_gate, grad_up, total, pieces):
    z = ids[2]
    pieces[0], pieces[1], pieces[2], pieces[3] = p0[...], p1[...], p2[...], p3[...]
    for zz in range(4):
        piece = pieces[zz ^ z].astype(f32)
        for at, grad in ((0, grad_gate), (nh * run, grad_up)):
            for k in range(nh):
                lo = (k * 4 + zz) * run
                grad[:, lo : lo + run] = piece[:, at + k * run : at + (k + 1) * run]
    both = grad_gate[...] * gate[...].astype(f32) + grad_up[...] * up[...].astype(f32)
    total[...] = jnp.sum(both, axis=1, keepdims=True)


def heads_kernel(nh, qw, vw, ids, p0, p1, p2, p3, wq, wk, wv, gq, gk, gv, total, pieces):
    h = ids[0]
    pieces[0], pieces[1], pieces[2], pieces[3] = p0[...], p1[...], p2[...], p3[...]
    for k in range(nh):
        piece = pieces[k ^ h].astype(f32)
        gq[:, k * qw : (k + 1) * qw] = piece[:, :qw]
        gk[:, k * qw : (k + 1) * qw] = piece[:, qw : 2 * qw]
        gv[:, k * vw : (k + 1) * vw] = piece[:, 2 * qw :]
    sums = [
        jnp.sum(g[...] * w[...].astype(f32), axis=1, keepdims=True)
        for g, w in ((gq, wq), (gk, wk), (gv, wv))
    ]
    total[...] = sums[0] + sums[1] + sums[2]


def call(body, ids, arrays, outs, scratch, room=6):
    vmem = pl.BlockSpec(memory_space=pltpu.VMEM)
    held = list(arrays) + jax.tree.leaves(outs) + list(scratch)
    held = sum(math.prod(x.shape[:-1]) * max(x.shape[-1], 128) * x.dtype.itemsize for x in held)
    return pl.pallas_call(
        body,
        out_shape=outs,
        in_specs=[pl.BlockSpec(memory_space=pltpu.SMEM)] + [vmem] * len(arrays),
        out_specs=jax.tree.map(lambda _: vmem, outs),
        scratch_shapes=scratch,
        compiler_params=pltpu.CompilerParams(vmem_limit_bytes=held + room * 1024 * 1024),
    )(ids, *arrays)


def shards(
    tokens,
    cotangent,
    teacher,
    lengths,
    gain_attn,
    gain_mlp,
    w_query,
    w_key,
    w_value,
    w_out,
    w_gate,
    w_up,
    w_down,
):
    seqs, slot, width = tokens.shape
    cores = lax.axis_size("c")
    nh, nb = lax.axis_size(HEAD), 4 * cores
    h, b = lax.axis_index(HEAD), lax.axis_index(BLK)
    hd = H // nh
    pairs = seqs * hd
    copies = nb // pairs
    drow = w_query.shape[0]
    fw, vw = w_query.shape[1] // H, w_value.shape[1] // H
    pw = 2 * fw + vw
    ffl = w_gate.shape[1] // 4
    lanes = nh * slot
    sb = min(512, nb * slot)
    n = nb * slot * nh // sb
    ids = jnp.stack([h, b, lax.axis_index(LINE)]).astype(jnp.int32)

    def columns(ws):
        return jnp.concatenate([w.reshape(drow, nh, -1).transpose(1, 0, 2) for w in ws], axis=2)

    def gathered(x):
        return lax.all_gather(x[None], CROSS, axis=0, tiled=True)

    def summed(shares):
        return lax.psum_scatter(shares, CROSS, scatter_dimension=0)

    qkv_cols = columns((w_query, w_key, w_value))
    run = w_gate.shape[1] // (4 * nh)
    feed = jax.ShapeDtypeStruct((4, drow, 2 * ffl), bf16)
    ffn_cols = call(functools.partial(cut_kernel, nh, run), ids, [w_gate, w_up], feed, [])

    place = (h * nb + b) * slot + lax.broadcasted_iota(jnp.int32, (seqs, slot), 1)
    valid = (place < lengths[:, None]).astype(f32)[..., None]
    count = jnp.sum(lengths).astype(f32)

    tokens_f = tokens.astype(f32)
    scale_one = rms_scale(tokens_f)
    own_rows = (tokens_f * scale_one * gain_attn).astype(bf16)
    (*got, ffn_1, ffn_2), (own_rows,) = window(
        turn_moves(qkv_cols, HEAD) + [(ffn_cols[1], LINE, 1), (ffn_cols[2], LINE, 2)], (own_rows,)
    )
    qkv_cols = turned(qkv_cols, got, HEAD)
    (row_1, row_2, qkv_near, qkv_far), _ = window(
        [(own_rows, HEAD, 1), (own_rows, HEAD, 2), (qkv_cols, LINE, 1), (qkv_cols, LINE, 2)]
    )
    (row_3, qkv_last, out_near, out_far), _ = window(
        [(own_rows, HEAD, 3), (qkv_far, LINE, 1), (w_out, LINE, 1), (w_out, LINE, 2)]
    )
    attn_rows = [own_rows, row_1, row_2, row_3]
    qkv_w = line_whole([qkv_cols, qkv_near, qkv_far, qkv_last])
    (*got, out_last), _ = window(over(qkv_w, "c") + [(out_far, LINE, 1)])
    qkv_w = core_end(qkv_w, got).transpose(2, 0, 1, 3, 4).reshape(width, -1)
    out_w = line_whole([w_out, out_near, out_far, out_last])
    normed_attn = jnp.concatenate(attn_rows, axis=1).reshape(-1, width)
    geometry = (nh, nb, slot, sb)
    piece = lambda rows: jax.ShapeDtypeStruct((cores, 4, rows, lanes), bf16)
    held = lambda rows: [pltpu.VMEM((pairs, rows, lanes), bf16)]
    taken = lambda rows: [pltpu.VMEM((nb, rows, lanes), bf16)]
    own_part = jax.ShapeDtypeStruct((seqs, slot, width), f32)
    sent_part = jax.ShapeDtypeStruct((3, seqs, slot, width), bf16)
    pieces = call(
        functools.partial(qkv_kernel, hd, copies, fw, vw),
        ids,
        attn_rows + [qkv_w],
        piece(pw),
        held(pw),
        room=10,
    )
    pieces, out_w = tie(pieces, out_w)
    sent, got, (ffn_last, down_w) = exchange(
        pieces, far_moves=over(out_w, "c"), far_beside=(ffn_cols[3], gathered(w_down))
    )
    down_w = down_w.reshape(-1, width)
    ffn_3 = swap(ffn_last, LINE, 3)
    out_w = core_end(out_w, got).reshape(-1, width)
    tiles, res, mixed_out = call(
        functools.partial(fwd_kernel, *geometry),
        ids,
        sent,
        [
            jax.ShapeDtypeStruct((n, pw, sb), bf16),
            jax.ShapeDtypeStruct((n, sb, 128), f32),
            piece(vw),
        ],
        [pltpu.VMEM((n, sb, 128), bf16)],
        room=14,
    )
    mixed_out, ffn_3 = tie(mixed_out, ffn_3)
    ffn_w = gathered(line_whole([ffn_cols[0], ffn_1, ffn_2, ffn_3]))
    ffn_w = ffn_w.reshape(nh, cores, 4, drow, -1).transpose(0, 2, 1, 3, 4).reshape(width, -1)
    mixed, attn_own, attn_part = call(
        functools.partial(out_kernel, hd, copies),
        ids,
        exchange(mixed_out)[0] + [out_w],
        [jax.ShapeDtypeStruct((hd * vw, seqs * lanes), bf16), own_part, sent_part],
        taken(vw),
        room=10,
    )
    got, _ = window([(attn_part[o - 1], HEAD, o) for o in range(1, 4)])
    residual = tokens_f + plus(attn_own, got)

    scale_two = rms_scale(residual)
    own_rows = (residual * scale_two * gain_mlp).astype(bf16)

    def forward(*rows):
        both = dot(jnp.concatenate([x.reshape(-1, width) for x in rows]), ffn_w, 1, 0)
        gate, up = both[:, :ffl], both[:, ffl:]
        hidden = (jax.nn.silu(gate) * up).astype(bf16)
        part = dot(hidden, down_w, 1, 0).reshape(len(rows), seqs, slot, width)
        return gate, up, hidden, part

    (near, far), (ffn_w,) = window([(own_rows, LINE, 1), (own_rows, LINE, 2)], (ffn_w,))
    (last,), first = window([(far, LINE, 1)], forward(own_rows, near, far))
    kept = [first, forward(last)]
    part = [y for x in kept for y in x[3]]
    normed_mlp = jnp.concatenate([x.reshape(-1, width) for x in (own_rows, near, far, last)])
    hidden = jnp.concatenate([x[2] for x in kept])
    passing = swap(part[3].astype(bf16), LINE, 1)
    got, _ = window(rest_moves([x.astype(bf16) for x in part], passing))
    full = valid * (residual + plus(part[0], got))
    diff = full - teacher.astype(f32)
    (loss,) = tie(jnp.full((1, 64, 128), jnp.sum(valid * diff * diff)))
    loss = lax.all_gather(loss, AXES, axis=0, tiled=True)

    grad_res = valid * (cotangent.astype(f32) + 2.0 * valid * diff / (width * count))
    own_rows = grad_res.astype(bf16)

    def backward(rows, gate, up):
        grad_hidden = dot(jnp.concatenate([x.reshape(-1, width) for x in rows]), down_w, 1, 1)
        sigma = jax.nn.sigmoid(gate)
        slope = sigma * (1.0 + gate * (1.0 - sigma))
        grad_gate = (grad_hidden * up * slope).astype(bf16)
        grad_up = (grad_hidden * gate * sigma).astype(bf16)
        grad_both = jnp.concatenate([grad_gate, grad_up], axis=1)
        return grad_both, dot(grad_both, ffn_w, 1, 1).reshape(len(rows), seqs, slot, width)

    def norm_back(grad_norm, values, scale_rows, gain):
        unit = values * scale_rows
        e = grad_norm * gain
        return scale_rows * (e - unit * jnp.mean(e * unit, axis=-1, keepdims=True))

    (near, far), _ = window([(own_rows, LINE, 1), (own_rows, LINE, 2)])
    (last,), first = window([(far, LINE, 1)], backward((own_rows, near, far), *kept[0][:2]))
    back = [first, backward((last,), *kept[1][:2])]
    part = [y for x in back for y in x[1]]
    passing = swap(part[3].astype(bf16), LINE, 1)
    grad_both = jnp.concatenate([x[0] for x in back])
    grad_ffn = jnp.concatenate([x.reshape(-1, width) for x in (own_rows, near, far, last)])
    part, grad_both, hidden = tie(part, grad_both, hidden)
    grad_down = dot(hidden, grad_ffn, 0, 0).astype(bf16).reshape(nb, -1, width)
    passing, grad_down, normed_mlp = tie(passing, grad_down, normed_mlp)
    grad_down = summed(grad_down)
    grad_ffn_w = dot(normed_mlp, grad_both, 0, 0).astype(bf16)
    grad_ffn_w = grad_ffn_w.reshape(nh, 4, cores, drow, -1).transpose(0, 2, 1, 3, 4)
    shares = grad_ffn_w.reshape(nb, 4 * drow, -1)
    got, (shares, loss) = window(rest_moves([x.astype(bf16) for x in part], passing), (shares, loss))
    grad_ffn_w = summed(shares)
    loss = jnp.sum(loss[:, 0, 0]) / (width * count)
    grad_resid = grad_res + norm_back(plus(part[0], got), residual, scale_two, gain_mlp)
    own_rows = grad_resid.astype(bf16)
    got, _ = window(over(own_rows, HEAD))
    sent, grad_out_w = call(
        functools.partial(mixed_back_kernel, hd, copies),
        ids,
        [own_rows] + got + [out_w, mixed],
        [piece(vw), jax.ShapeDtypeStruct((cores, 4, drow, width), bf16)],
        held(vw),
        room=10,
    )
    sent, out_got, _ = exchange(
        sent, far_moves=[(grad_out_w[k], "c", k) for k in range(1, cores)]
    )
    grad_out_w = plus(grad_out_w[0], out_got).astype(bf16)
    sent, grad_out_w = tie(sent, grad_out_w)
    out_got = [swap(grad_out_w[o], LINE, o) for o in range(1, 3)]
    grads_out = call(
        functools.partial(bwd_kernel, *geometry),
        ids,
        [tiles, res] + sent,
        piece(pw),
        [
            pltpu.VMEM((n, vw, sb), bf16),
            pltpu.VMEM((n, sb, fw), bf16),
            pltpu.VMEM((n, pw, sb), f32),
        ],
        room=14,
    )
    grads_out, out_got = tie(grads_out, out_got)
    grad_qkv, _, (grad_ffn_w,) = exchange(grads_out, far_beside=(grad_ffn_w,))
    grad_ffn_w = grad_ffn_w.reshape(4, drow, -1)
    ffn_pieces = [pick(grad_ffn_w, lax.axis_index(LINE) ^ o) for o in range(4)]
    grad_qkv_w, own_back, attn_back = call(
        functools.partial(qkv_back_kernel, hd, copies, fw, vw),
        ids,
        grad_qkv + [normed_attn, qkv_w],
        [jax.ShapeDtypeStruct((cores, 4, nh, drow, hd * pw), bf16), own_part, sent_part],
        taken(pw) + [pltpu.VMEM((hd * pw, seqs * lanes), bf16)],
        room=14,
    )
    row_moves = [(attn_back[o - 1], HEAD, o) for o in range(1, 4)]
    got, _ = window([(grad_qkv_w[k], "c", k) for k in range(1, cores)])
    grad_qkv_w = plus(grad_qkv_w[0], got).astype(bf16)
    (passing, ffn_2, *row_got), _ = window(
        [by_way(grad_qkv_w), (ffn_pieces[2], LINE, 2)] + row_moves[:2]
    )
    (got_1, got_2, last, ffn_3), _ = window(
        rest_moves(grad_qkv_w, passing) + [row_moves[2], (ffn_pieces[3], LINE, 3)]
    )
    row_got = row_got + [last]
    grad_qkv_w = plus(grad_qkv_w[0], [got_1, got_2]).astype(bf16)
    (*got, ffn_1, out_last), _ = window(
        turn_moves(grad_qkv_w, HEAD) + [(ffn_pieces[1], LINE, 1), (grad_out_w[3], LINE, 3)]
    )
    out_got = out_got + [out_last]
    grad_down, got = tie(grad_down, got)
    rows_f32 = lambda w: jax.ShapeDtypeStruct(w.shape, f32)
    one = jax.ShapeDtypeStruct((drow, 1), f32)
    gg, gu, gain_sum_two = call(
        functools.partial(feed_kernel, nh, run),
        ids,
        [ffn_pieces[0], ffn_1, ffn_2, ffn_3, w_gate, w_up],
        [rows_f32(w_gate), rows_f32(w_up), one],
        [pltpu.VMEM((4, drow, 2 * ffl), bf16)],
    )
    gq, gk, gv, gain_sum_one = call(
        functools.partial(heads_kernel, nh, hd * fw, hd * vw),
        ids,
        [pick(grad_qkv_w, h)] + got + [w_query, w_key, w_value],
        [rows_f32(w_query), rows_f32(w_key), rows_f32(w_value), one],
        [pltpu.VMEM((4, drow, hd * pw), bf16)],
    )
    grad_out_w = plus(grad_out_w[0], out_got)
    grad_in = plus(own_back, row_got)
    grad_tokens = grad_resid + norm_back(grad_in, tokens_f, scale_one, gain_attn)

    def gain_grad(total, gain):
        at = lax.axis_index(AXES) * drow
        return total[:, 0] / lax.dynamic_slice(gain, (at,), (drow,))

    return (
        full.astype(bf16),
        loss,
        grad_tokens,
        gq,
        gk,
        gv,
        grad_out_w.astype(f32),
        gg,
        gu,
        grad_down.astype(f32),
        gain_grad(gain_sum_one, gain_attn),
        gain_grad(gain_sum_two, gain_mlp),
    )


def solution(mesh):
    parts = Mesh(mesh.devices.reshape(mesh.shape["head"], 4, -1), AXES)
    rows, slots = P(AXES, None), P(None, AXES, None)
    return jax.shard_map(
        shards,
        mesh=parts,
        in_specs=(slots,) * 3 + (P(),) * 3 + (rows,) * 7,
        out_specs=(slots, P(), slots) + (rows,) * 7 + (P(AXES),) * 2,
        check_vma=False,
    )
```

```python
import functools
import math

import jax
import jax.numpy as jnp
from jax import lax
from jax.experimental import pallas as pl
from jax.experimental.pallas import tpu as pltpu
from jax.sharding import Mesh
from jax.sharding import PartitionSpec as P

H = 16
norm_eps = 1e-06
bf16, f32 = jnp.bfloat16, jnp.float32


def dot(a, b, ca, cb):
    return lax.dot_general(a, b, (((ca,), (cb,)), ((), ())), preferred_element_type=f32)


def swap(x, axis, o):
    n = lax.axis_size(axis)
    return lax.ppermute(x, axis, [(i, i ^ o) for i in range(n)])


def rms_scale(values):
    return lax.rsqrt(jnp.mean(values * values, axis=-1, keepdims=True) + norm_eps)


HEAD, LINE, BLK, CROSS = "head", "z", ("z", "c"), ("head", "c")
AXES = (HEAD,) + BLK


def tie(*values):
    return lax.optimization_barrier(values)


def window(moves, beside=()):
    arrays = tie(*[x for x, _, _ in moves])
    return tie([swap(x, axis, o) for x, (_, axis, o) in zip(arrays, moves)], beside)


def over(x, axis):
    return [(x, axis, o) for o in range(1, lax.axis_size(axis))]


def turn_moves(pieces, axis):
    me = lax.axis_index(axis)
    return [(pick(pieces, me ^ o), axis, o) for o in range(1, lax.axis_size(axis))]


def turned(pieces, got, axis):
    me = lax.axis_index(axis)
    return in_place([pick(pieces, me)] + list(got), me)


def return_moves(parts, axis):
    return [(x, axis, o) for o, x in enumerate(parts) if o]


def plus(own, got):
    return sum([x.astype(f32) for x in got], own.astype(f32))


def by_way(blocks):
    return (blocks[3], LINE, 1)


def rest_moves(blocks, passing):
    far = (blocks[2].astype(f32) + passing.astype(f32)).astype(bf16)
    return [(blocks[1], LINE, 1), (far, LINE, 2)]


def exchange(pieces, far_moves=(), far_beside=()):
    got, _ = window([(pieces[k], "c", k) for k in range(1, pieces.shape[0])])
    near = jnp.stack([pieces[0]] + got, axis=1)
    got, far_beside = window([(near[o], LINE, o) for o in range(1, 4)] + list(far_moves), far_beside)
    return [near[0]] + got[:3], got[3:], far_beside


def in_place(got, me):
    whole = jnp.zeros((len(got),) + got[0].shape, got[0].dtype)
    for o, x in enumerate(got):
        whole = lax.dynamic_update_index_in_dim(whole, x, me ^ o, 0)
    return whole


def pick(x, i, axis=0):
    return lax.dynamic_index_in_dim(x, i, axis, keepdims=False)


def line_whole(got):
    return in_place(got, lax.axis_index(LINE))


def core_end(own, got):
    return jnp.moveaxis(in_place([own] + list(got), lax.axis_index("c")), 0, 1)


def core_share(parts, at):
    me = lax.axis_index("c")
    return [(pick(parts, me ^ o, at), "c", o) for o in range(1, lax.axis_size("c"))]


def core_sum(parts, got, at):
    return plus(pick(parts, lax.axis_index("c"), at), got).astype(bf16)


def line_blocks(near, at):
    return [pick(near, lax.axis_index(LINE) ^ o, at) for o in range(4)]


def positions(b, sub, cps, slot, dim, sb):
    shape = (sb, 1) if dim == 0 else (1, sb)
    lane = lax.broadcasted_iota(jnp.int32, shape, dim)
    return ((b ^ (sub * cps + lane // slot)) * slot) + lane % slot


def flip(x):
    return jnp.transpose(x.astype(f32)).astype(bf16)


def kernel_sum(score):
    lifted = score + 4.0
    return lifted * lifted * (1.0 / 32.0) + 0.5


def fwd_kernel(nh, nb, slot, sb, ids, got0, got1, got2, got3, tiles, res, out, vrow):
    got, cores = (got0, got1, got2, got3), nb // 4
    nsub, cps = nb * slot // sb, sb // slot
    h, b = ids[0], ids[1]
    for o in range(nb):
        for oh in range(nh):
            at = (h ^ oh) * nsub + o // cps
            lo = (o % cps) * slot
            piece = got[o // cores][o % cores, :, oh * slot : (oh + 1) * slot]
            tiles[at, :, lo : lo + slot] = piece

    def rows_of(i, c):
        vv = jnp.concatenate([tiles[i, 32:144, :].astype(f32), jnp.ones((16, sb), f32)], axis=0)
        vrow[i] = jnp.transpose(vv).astype(bf16)
        return c

    lax.fori_loop(0, nh * nsub, rows_of, 0)

    for oh in range(nh):
        hq = h ^ oh
        for sub in range(nsub):
            iq = hq * nsub + sub
            qrow = flip(tiles[iq, 0:16, :])
            pos_q = positions(b, sub, cps, slot, 0, sb)

            def step(ik, acc, masked):
                w = kernel_sum(dot(qrow, tiles[ik, 16:32, :], 1, 0))
                if masked:
                    pos_k = positions(b, ik - hq * nsub, cps, slot, 1, sb)
                    w = jnp.where(pos_q >= pos_k, w, 0.0)
                return acc + dot(w.astype(bf16), vrow[ik], 1, 0)

            acc = lax.fori_loop(
                0, hq * nsub, functools.partial(step, masked=False), jnp.zeros((sb, 128), f32)
            )
            acc = lax.fori_loop(hq * nsub, (hq + 1) * nsub, functools.partial(step, masked=True), acc)
            den = acc[:, 112:113]
            mixed = acc / den
            lane = lax.broadcasted_iota(jnp.int32, (sb, 128), 1)
            res[iq] = jnp.where(lane == 112, den, mixed)
            back = jnp.transpose(mixed)[0:112].astype(bf16)
            for c in range(cps):
                o = sub * cps + c
                piece = back[:, c * slot : (c + 1) * slot]
                out[o % cores, o // cores, :, oh * slot : (oh + 1) * slot] = piece


def bwd_kernel(nh, nb, slot, sb, ids, tiles, res, got0, got1, got2, got3, out, gt, krow, acc):
    got, cores = (got0, got1, got2, got3), nb // 4
    nsub, cps = nb * slot // sb, sb // slot
    h, b = ids[0], ids[1]
    for o in range(nb):
        for oh in range(nh):
            at = (h ^ oh) * nsub + o // cps
            lo = (o % cps) * slot
            piece = got[o // cores][o % cores, :, oh * slot : (oh + 1) * slot]
            gt[at, :, lo : lo + slot] = piece

    def rows_of(i, c):
        krow[i] = flip(tiles[i, 16:32, :])
        acc[i] = jnp.zeros((144, sb), f32)
        return c

    lax.fori_loop(0, nh * nsub, rows_of, 0)

    for oh in range(nh):
        hq = h ^ oh
        for sub in range(nsub):
            iq = hq * nsub + sub
            qcol = tiles[iq, 0:16, :]
            qrow = flip(qcol)
            gcol = gt[iq]
            grow = jnp.transpose(gcol.astype(f32))
            kept = res[iq]
            rden = 1.0 / kept[:, 112:113]
            delta = jnp.sum(grow * kept[:, 0:112], axis=1, keepdims=True)
            grow = grow.astype(bf16)
            pos_q = positions(b, sub, cps, slot, 0, sb)

            def step(ik, dq, masked):
                lifted = dot(qrow, tiles[ik, 16:32, :], 1, 0) + 4.0
                g = (dot(grow, tiles[ik, 32:144, :], 1, 0) - delta) * rden
                p = (lifted * lifted * (1.0 / 32.0) + 0.5) * rden
                ds = g * lifted * (1.0 / 16.0)
                if masked:
                    pos_k = positions(b, ik - hq * nsub, cps, slot, 1, sb)
                    keep = pos_q >= pos_k
                    p = jnp.where(keep, p, 0.0)
                    ds = jnp.where(keep, ds, 0.0)
                p, ds = p.astype(bf16), ds.astype(bf16)
                acc[ik, 32:144, :] += dot(gcol, p, 1, 0)
                acc[ik, 16:32, :] += dot(qcol, ds, 1, 0)
                return dq + dot(ds, krow[ik], 1, 0)

            dq = lax.fori_loop(
                0, hq * nsub, functools.partial(step, masked=False), jnp.zeros((sb, 16), f32)
            )
            dq = lax.fori_loop(hq * nsub, (hq + 1) * nsub, functools.partial(step, masked=True), dq)
            acc[iq, 0:16, :] = jnp.transpose(dq)
    for oh in range(nh):
        for o in range(nb):
            at = (h ^ oh) * nsub + o // cps
            lo = (o % cps) * slot
            piece = acc[at, :, lo : lo + slot].astype(bf16)
            out[o % cores, o // cores, :, oh * slot : (oh + 1) * slot] = piece


def rows_of(refs, s):
    return jnp.concatenate([x[s] for x in refs], axis=0)


def to_peers(cores, copies, b, pieces, out):
    for o in range(4 * cores):
        out[o % cores, o // cores] = pieces[(b ^ o) // copies]


def from_peers(cores, copies, b, got, pieces):
    for o in range(4 * cores):
        pieces[o] = got[o // cores][o % cores]
    return lambda p: pieces[b ^ (p * copies)]


def qkv_kernel(hd, copies, fw, vw, ids, x0, x1, x2, x3, w, out, pieces):
    cores = out.shape[0]
    for s in range(x0.shape[0]):
        rows = jnp.dot(rows_of((x0, x1, x2, x3), s), w[...], preferred_element_type=f32)
        cols = jnp.transpose(rows)
        for j in range(hd):
            at = (j * fw, (hd + j) * fw, 2 * hd * fw + j * vw)
            piece = [cols[lo : lo + n] for lo, n in zip(at, (fw, fw, vw))]
            pieces[s * hd + j] = jnp.concatenate(piece, axis=0).astype(bf16)
    to_peers(cores, copies, ids[1], pieces, out)


def out_kernel(hd, copies, ids, g0, g1, g2, g3, w, mixed, own, send, pieces):
    cores, vw, lanes = g0.shape
    seqs, slot = own.shape[:2]
    take = from_peers(cores, copies, ids[1], (g0, g1, g2, g3), pieces)
    for s in range(seqs):
        cols = jnp.concatenate([take(s * hd + j) for j in range(hd)], axis=0)
        mixed[:, s * lanes : (s + 1) * lanes] = cols
        rows = jnp.transpose(cols.astype(f32)).astype(bf16)
        part = jnp.dot(rows, w[...], preferred_element_type=f32)
        own[s] = part[:slot]
        for o in range(1, 4):
            send[o - 1, s] = part[o * slot : (o + 1) * slot].astype(bf16)


def mixed_back_kernel(hd, copies, ids, x0, x1, x2, x3, w, mixed, out, grad, pieces):
    cores, vw, lanes = out.shape[0], out.shape[2], out.shape[3]
    z, c = ids[2], ids[1] % cores
    rows = [rows_of((x0, x1, x2, x3), s) for s in range(x0.shape[0])]
    for s, x in enumerate(rows):
        cols = dot(w[...], x, 1, 1)
        for j in range(hd):
            pieces[s * hd + j] = cols[j * vw : (j + 1) * vw].astype(bf16)
    to_peers(cores, copies, ids[1], pieces, out)
    total = jnp.dot(mixed[...], jnp.concatenate(rows, axis=0), preferred_element_type=f32)
    drow = grad.shape[2]
    for k in range(4 * cores):
        grad[(k % cores) ^ c, (k // cores) ^ z] = total[k * drow : (k + 1) * drow].astype(bf16)


def qkv_back_kernel(
    hd, copies, fw, vw, ids, g0, g1, g2, g3, x0, x1, x2, x3, w, grad, own, send, pieces, cols
):
    cores, pw, lanes = g0.shape
    seqs, slot = own.shape[:2]
    z, c = ids[2], ids[1] % cores
    take = from_peers(cores, copies, ids[1], (g0, g1, g2, g3), pieces)
    for s in range(seqs):
        for j in range(hd):
            piece = take(s * hd + j)
            at = (j * fw, (hd + j) * fw, 2 * hd * fw + j * vw)
            lo = 0
            for row, n in zip(at, (fw, fw, vw)):
                cols[row : row + n, s * lanes : (s + 1) * lanes] = piece[lo : lo + n]
                lo += n
    rows = jnp.transpose(cols[...].astype(f32)).astype(bf16)
    for s in range(seqs):
        part = dot(rows[s * lanes : (s + 1) * lanes], w[...], 1, 1)
        own[s] = part[:slot]
        for o in range(1, 4):
            send[o - 1, s] = part[o * slot : (o + 1) * slot].astype(bf16)
    x = jnp.concatenate([rows_of((x0, x1, x2, x3), s) for s in range(seqs)], axis=0)
    drow, half = grad.shape[3], x.shape[1] // 2
    for i in range(2):
        total = dot(x[:, i * half : (i + 1) * half], rows, 0, 0)
        for k in range(half // drow):
            at = i * (half // drow) + k
            block = total[k * drow : (k + 1) * drow].astype(bf16)
            grad[(at % cores) ^ c, (at // cores % 4) ^ z, at // (4 * cores)] = block


def cut_kernel(nh, run, ids, gate, up, wq, wk, wv, out, heads):
    h, z = ids[0], ids[2]
    qw, vw = wq.shape[1] // nh, wv.shape[1] // nh
    for k in range(nh):
        parts = [wq[:, k * qw : (k + 1) * qw], wk[:, k * qw : (k + 1) * qw]]
        parts.append(wv[:, k * vw : (k + 1) * vw])
        heads[k ^ h] = jnp.concatenate([x.astype(f32) for x in parts], axis=1).astype(bf16)
    for zz in range(4):
        parts = []
        for w in (gate, up):
            parts += [w[:, (k * 4 + zz) * run : (k * 4 + zz + 1) * run] for k in range(nh)]
        out[zz ^ z] = jnp.concatenate([x.astype(f32) for x in parts], axis=1).astype(bf16)


def feed_kernel(nh, run, ids, p0, p1, p2, p3, gate, up, grad_gate, grad_up, total, pieces):
    z = ids[2]
    pieces[0], pieces[1], pieces[2], pieces[3] = p0[...], p1[...], p2[...], p3[...]
    for zz in range(4):
        piece = pieces[zz ^ z].astype(f32)
        for at, grad in ((0, grad_gate), (nh * run, grad_up)):
            for k in range(nh):
                lo = (k * 4 + zz) * run
                grad[:, lo : lo + run] = piece[:, at + k * run : at + (k + 1) * run]
    both = grad_gate[...] * gate[...].astype(f32) + grad_up[...] * up[...].astype(f32)
    total[...] = jnp.sum(both, axis=1, keepdims=True)


def heads_kernel(nh, qw, vw, ids, p0, p1, p2, p3, wq, wk, wv, gq, gk, gv, total, pieces):
    h = ids[0]
    pieces[0], pieces[1], pieces[2], pieces[3] = p0[...], p1[...], p2[...], p3[...]
    for k in range(nh):
        piece = pieces[k ^ h].astype(f32)
        gq[:, k * qw : (k + 1) * qw] = piece[:, :qw]
        gk[:, k * qw : (k + 1) * qw] = piece[:, qw : 2 * qw]
        gv[:, k * vw : (k + 1) * vw] = piece[:, 2 * qw :]
    sums = [
        jnp.sum(g[...] * w[...].astype(f32), axis=1, keepdims=True)
        for g, w in ((gq, wq), (gk, wk), (gv, wv))
    ]
    total[...] = sums[0] + sums[1] + sums[2]


def call(body, ids, arrays, outs, scratch, room=6):
    vmem = pl.BlockSpec(memory_space=pltpu.VMEM)
    held = list(arrays) + jax.tree.leaves(outs) + list(scratch)
    held = sum(math.prod(x.shape[:-1]) * max(x.shape[-1], 128) * x.dtype.itemsize for x in held)
    return pl.pallas_call(
        body,
        out_shape=outs,
        in_specs=[pl.BlockSpec(memory_space=pltpu.SMEM)] + [vmem] * len(arrays),
        out_specs=jax.tree.map(lambda _: vmem, outs),
        scratch_shapes=scratch,
        compiler_params=pltpu.CompilerParams(vmem_limit_bytes=held + room * 1024 * 1024),
    )(ids, *arrays)


def shards(
    tokens,
    cotangent,
    teacher,
    lengths,
    gain_attn,
    gain_mlp,
    w_query,
    w_key,
    w_value,
    w_out,
    w_gate,
    w_up,
    w_down,
):
    seqs, slot, width = tokens.shape
    cores = lax.axis_size("c")
    nh, nb = lax.axis_size(HEAD), 4 * cores
    h, b = lax.axis_index(HEAD), lax.axis_index(BLK)
    hd = H // nh
    pairs = seqs * hd
    copies = nb // pairs
    drow = w_query.shape[0]
    fw, vw = w_query.shape[1] // H, w_value.shape[1] // H
    pw = 2 * fw + vw
    ffl = w_gate.shape[1] // 4
    lanes = nh * slot
    sb = min(512, nb * slot)
    n = nb * slot * nh // sb
    ids = jnp.stack([h, b, lax.axis_index(LINE)]).astype(jnp.int32)

    def gathered(x):
        return lax.all_gather(x[None], CROSS, axis=0, tiled=True)

    def summed(shares):
        return lax.psum_scatter(shares, CROSS, scatter_dimension=0)

    run = w_gate.shape[1] // (4 * nh)
    ffn_cols, qkv_cols = call(
        functools.partial(cut_kernel, nh, run),
        ids,
        [w_gate, w_up, w_query, w_key, w_value],
        [
            jax.ShapeDtypeStruct((4, drow, 2 * ffl), bf16),
            jax.ShapeDtypeStruct((nh, drow, hd * pw), bf16),
        ],
        [],
    )

    place = (h * nb + b) * slot + lax.broadcasted_iota(jnp.int32, (seqs, slot), 1)
    valid = (place < lengths[:, None]).astype(f32)[..., None]
    count = jnp.sum(lengths).astype(f32)

    tokens_f = tokens.astype(f32)
    scale_one = rms_scale(tokens_f)
    own_rows = (tokens_f * scale_one * gain_attn).astype(bf16)
    (*got, ffn_1, ffn_2), (own_rows,) = window(
        return_moves(qkv_cols, HEAD) + [(ffn_cols[1], LINE, 1), (ffn_cols[2], LINE, 2)], (own_rows,)
    )
    qkv_cols = in_place([qkv_cols[0]] + got, h)
    (row_1, row_2, qkv_near, qkv_far), _ = window(
        [(own_rows, HEAD, 1), (own_rows, HEAD, 2), (qkv_cols, LINE, 1), (qkv_cols, LINE, 2)]
    )
    (row_3, qkv_last, ffn_3), _ = window(
        [(own_rows, HEAD, 3), (qkv_far, LINE, 1), (ffn_cols[3], LINE, 3)]
    )
    attn_rows = [own_rows, row_1, row_2, row_3]
    qkv_w = line_whole([qkv_cols, qkv_near, qkv_far, qkv_last])
    got, (ffn_cols,) = window(
        over(qkv_w, "c"), (line_whole([ffn_cols[0], ffn_1, ffn_2, ffn_3]),)
    )
    ffn_w = gathered(ffn_cols)
    ffn_w = ffn_w.reshape(nh, cores, 4, drow, -1).transpose(0, 2, 1, 3, 4).reshape(width, -1)
    qkv_w = core_end(qkv_w, got).transpose(2, 0, 1, 3, 4).reshape(width, -1)
    geometry = (nh, nb, slot, sb)
    piece = lambda rows: jax.ShapeDtypeStruct((cores, 4, rows, lanes), bf16)
    held = lambda rows: [pltpu.VMEM((pairs, rows, lanes), bf16)]
    taken = lambda rows: [pltpu.VMEM((nb, rows, lanes), bf16)]
    own_part = jax.ShapeDtypeStruct((seqs, slot, width), f32)
    sent_part = jax.ShapeDtypeStruct((3, seqs, slot, width), bf16)
    pieces = call(
        functools.partial(qkv_kernel, hd, copies, fw, vw),
        ids,
        attn_rows + [qkv_w],
        piece(pw),
        held(pw),
        room=10,
    )
    sent, _, (down_w, w_out_late) = exchange(pieces, far_beside=(gathered(w_down), w_out))
    down_w = down_w.reshape(-1, width)
    out_near, out_far = swap(w_out_late, LINE, 1), swap(w_out_late, LINE, 2)
    tiles, res, mixed_out = call(
        functools.partial(fwd_kernel, *geometry),
        ids,
        sent,
        [
            jax.ShapeDtypeStruct((n, pw, sb), bf16),
            jax.ShapeDtypeStruct((n, sb, 128), f32),
            piece(vw),
        ],
        [pltpu.VMEM((n, sb, 128), bf16)],
        room=14,
    )
    mixed_out, out_near, out_far = tie(mixed_out, out_near, out_far)
    mixed_got, (out_last,), _ = exchange(mixed_out, far_moves=[(out_far, LINE, 1)])
    out_w = line_whole([w_out, out_near, out_far, out_last])
    got, (out_w,) = window(over(out_w, "c"), (out_w,))
    out_w = core_end(out_w, got).reshape(-1, width)
    mixed, attn_own, attn_part = call(
        functools.partial(out_kernel, hd, copies),
        ids,
        mixed_got + [out_w],
        [jax.ShapeDtypeStruct((hd * vw, seqs * lanes), bf16), own_part, sent_part],
        taken(vw),
        room=10,
    )
    got, (ffn_w,) = window([(attn_part[o - 1], HEAD, o) for o in range(1, 4)], (ffn_w,))
    residual = tokens_f + plus(attn_own, got)

    scale_two = rms_scale(residual)
    own_rows = (residual * scale_two * gain_mlp).astype(bf16)

    def forward(*rows):
        both = dot(jnp.concatenate([x.reshape(-1, width) for x in rows]), ffn_w, 1, 0)
        gate, up = both[:, :ffl], both[:, ffl:]
        hidden = (jax.nn.silu(gate) * up).astype(bf16)
        part = dot(hidden, down_w, 1, 0).reshape(len(rows), seqs, slot, width)
        return gate, up, hidden, part

    (near, far), first = window([(own_rows, LINE, 1), (own_rows, LINE, 2)], forward(own_rows))
    (last,), second = window([(far, LINE, 1)], forward(near, far))
    kept = [first, second, forward(last)]
    part = [y for x in kept for y in x[3]]
    normed_mlp = jnp.concatenate([x.reshape(-1, width) for x in (own_rows, near, far, last)])
    hidden = jnp.concatenate([x[2] for x in kept])
    passing = swap(part[3].astype(bf16), LINE, 1)
    got, _ = window(rest_moves([x.astype(bf16) for x in part], passing))
    full = valid * (residual + plus(part[0], got))
    diff = full - teacher.astype(f32)
    (loss,) = tie(jnp.full((1, 64, 128), jnp.sum(valid * diff * diff)))
    loss = lax.all_gather(loss, AXES, axis=0, tiled=True)

    grad_res = valid * (cotangent.astype(f32) + 2.0 * valid * diff / (width * count))
    own_rows = grad_res.astype(bf16)

    def backward(rows, gate, up):
        grad_hidden = dot(jnp.concatenate([x.reshape(-1, width) for x in rows]), down_w, 1, 1)
        sigma = jax.nn.sigmoid(gate)
        slope = sigma * (1.0 + gate * (1.0 - sigma))
        grad_gate = (grad_hidden * up * slope).astype(bf16)
        grad_up = (grad_hidden * gate * sigma).astype(bf16)
        grad_both = jnp.concatenate([grad_gate, grad_up], axis=1)
        return grad_both, dot(grad_both, ffn_w, 1, 1).reshape(len(rows), seqs, slot, width)

    def norm_back(grad_norm, values, scale_rows, gain):
        unit = values * scale_rows
        e = grad_norm * gain
        return scale_rows * (e - unit * jnp.mean(e * unit, axis=-1, keepdims=True))

    (near, far), first = window(
        [(own_rows, LINE, 1), (own_rows, LINE, 2)], backward((own_rows,), *kept[0][:2])
    )
    (last,), second = window([(far, LINE, 1)], backward((near, far), *kept[1][:2]))
    back = [first, second, backward((last,), *kept[2][:2])]
    part = [y for x in back for y in x[1]]
    passing = swap(part[3].astype(bf16), LINE, 1)
    grad_both = jnp.concatenate([x[0] for x in back])
    grad_ffn = jnp.concatenate([x.reshape(-1, width) for x in (own_rows, near, far, last)])
    part, grad_both, hidden = tie(part, grad_both, hidden)
    grad_down = dot(hidden, grad_ffn, 0, 0).astype(bf16).reshape(nb, -1, width)
    passing, grad_down, normed_mlp = tie(passing, grad_down, normed_mlp)
    grad_down = summed(grad_down)
    grad_ffn_w = dot(normed_mlp, grad_both, 0, 0).astype(bf16)
    grad_ffn_w = grad_ffn_w.reshape(nh, 4, cores, drow, -1).transpose(0, 2, 1, 3, 4)
    shares = grad_ffn_w.reshape(nb, 4 * drow, -1)
    got, (shares, loss) = window(rest_moves([x.astype(bf16) for x in part], passing), (shares, loss))
    grad_ffn_w = summed(shares)
    loss = jnp.sum(loss[:, 0, 0]) / (width * count)
    grad_resid = grad_res + norm_back(plus(part[0], got), residual, scale_two, gain_mlp)
    own_rows = grad_resid.astype(bf16)
    got, _ = window(over(own_rows, HEAD))
    sent, grad_out_w = call(
        functools.partial(mixed_back_kernel, hd, copies),
        ids,
        [own_rows] + got + [out_w, mixed],
        [piece(vw), jax.ShapeDtypeStruct((cores, 4, drow, width), bf16)],
        held(vw),
        room=10,
    )
    sent, out_got, _ = exchange(
        sent, far_moves=[(grad_out_w[k], "c", k) for k in range(1, cores)]
    )
    grad_out_w = plus(grad_out_w[0], out_got).astype(bf16)
    sent, grad_out_w = tie(sent, grad_out_w)
    out_got = [swap(grad_out_w[o], LINE, o) for o in range(1, 4)]
    grads_out = call(
        functools.partial(bwd_kernel, *geometry),
        ids,
        [tiles, res] + sent,
        piece(pw),
        [
            pltpu.VMEM((n, vw, sb), bf16),
            pltpu.VMEM((n, sb, fw), bf16),
            pltpu.VMEM((n, pw, sb), f32),
        ],
        room=14,
    )
    grads_out, out_got = tie(grads_out, out_got)
    grad_qkv, _, (grad_ffn_w,) = exchange(grads_out, far_beside=(grad_ffn_w,))
    grad_qkv_w, own_back, attn_back = call(
        functools.partial(qkv_back_kernel, hd, copies, fw, vw),
        ids,
        grad_qkv + attn_rows + [qkv_w],
        [jax.ShapeDtypeStruct((cores, 4, nh, drow, hd * pw), bf16), own_part, sent_part],
        taken(pw) + [pltpu.VMEM((hd * pw, seqs * lanes), bf16)],
        room=14,
    )
    grad_qkv_w, grad_ffn_w = tie(grad_qkv_w, grad_ffn_w)
    grad_ffn_w = grad_ffn_w.reshape(4, drow, -1)
    ffn_pieces = [pick(grad_ffn_w, lax.axis_index(LINE) ^ o) for o in range(4)]
    row_moves = [(attn_back[o - 1], HEAD, o) for o in range(1, 4)]
    got, _ = window([(grad_qkv_w[k], "c", k) for k in range(1, cores)])
    grad_qkv_w = plus(grad_qkv_w[0], got).astype(bf16)
    (passing, ffn_2, *row_got), _ = window(
        [by_way(grad_qkv_w), (ffn_pieces[2], LINE, 2)] + row_moves[:2]
    )
    (got_1, got_2, last, ffn_1), _ = window(
        rest_moves(grad_qkv_w, passing) + [row_moves[2], (ffn_pieces[1], LINE, 1)]
    )
    row_got = row_got + [last]
    grad_qkv_w = plus(grad_qkv_w[0], [got_1, got_2]).astype(bf16)
    (*got, ffn_3), _ = window(turn_moves(grad_qkv_w, HEAD) + [(ffn_pieces[3], LINE, 3)])
    grad_down, got = tie(grad_down, got)
    rows_f32 = lambda w: jax.ShapeDtypeStruct(w.shape, f32)
    one = jax.ShapeDtypeStruct((drow, 1), f32)
    gg, gu, gain_sum_two = call(
        functools.partial(feed_kernel, nh, run),
        ids,
        [ffn_pieces[0], ffn_1, ffn_2, ffn_3, w_gate, w_up],
        [rows_f32(w_gate), rows_f32(w_up), one],
        [pltpu.VMEM((4, drow, 2 * ffl), bf16)],
    )
    gq, gk, gv, gain_sum_one = call(
        functools.partial(heads_kernel, nh, hd * fw, hd * vw),
        ids,
        [pick(grad_qkv_w, h)] + got + [w_query, w_key, w_value],
        [rows_f32(w_query), rows_f32(w_key), rows_f32(w_value), one],
        [pltpu.VMEM((4, drow, hd * pw), bf16)],
    )
    grad_out_w = plus(grad_out_w[0], out_got)
    grad_in = plus(own_back, row_got)
    grad_tokens = grad_resid + norm_back(grad_in, tokens_f, scale_one, gain_attn)

    def gain_grad(total, gain):
        at = lax.axis_index(AXES) * drow
        return total[:, 0] / lax.dynamic_slice(gain, (at,), (drow,))

    return (
        full.astype(bf16),
        loss,
        grad_tokens,
        gq,
        gk,
        gv,
        grad_out_w.astype(f32),
        gg,
        gu,
        grad_down.astype(f32),
        gain_grad(gain_sum_one, gain_attn),
        gain_grad(gain_sum_two, gain_mlp),
    )


def solution(mesh):
    parts = Mesh(mesh.devices.reshape(mesh.shape["head"], 4, -1), AXES)
    rows, slots = P(AXES, None), P(None, AXES, None)
    return jax.shard_map(
        shards,
        mesh=parts,
        in_specs=(slots,) * 3 + (P(),) * 3 + (rows,) * 7,
        out_specs=(slots, P(), slots) + (rows,) * 7 + (P(AXES),) * 2,
        check_vma=False,
    )
```

```python
import functools
import math

import jax
import jax.numpy as jnp
from jax import lax
from jax.experimental import pallas as pl
from jax.experimental.pallas import tpu as pltpu
from jax.sharding import Mesh
from jax.sharding import PartitionSpec as P

H = 16
norm_eps = 1e-06
bf16, f32 = jnp.bfloat16, jnp.float32


def dot(a, b, ca, cb):
    return lax.dot_general(a, b, (((ca,), (cb,)), ((), ())), preferred_element_type=f32)


def swap(x, axis, o):
    n = lax.axis_size(axis)
    return lax.ppermute(x, axis, [(i, i ^ o) for i in range(n)])


def rms_scale(values):
    return lax.rsqrt(jnp.mean(values * values, axis=-1, keepdims=True) + norm_eps)


HEAD, LINE, BLK, CROSS = "head", "z", ("z", "c"), ("head", "c")
AXES = (HEAD,) + BLK


def tie(*values):
    return lax.optimization_barrier(values)


def window(moves, beside=()):
    arrays = tie(*[x for x, _, _ in moves])
    return tie([swap(x, axis, o) for x, (_, axis, o) in zip(arrays, moves)], beside)


def over(x, axis):
    return [(x, axis, o) for o in range(1, lax.axis_size(axis))]


def turn_moves(pieces, axis):
    me = lax.axis_index(axis)
    return [(pick(pieces, me ^ o), axis, o) for o in range(1, lax.axis_size(axis))]


def turned(pieces, got, axis):
    me = lax.axis_index(axis)
    return in_place([pick(pieces, me)] + list(got), me)


def return_moves(parts, axis):
    return [(x, axis, o) for o, x in enumerate(parts) if o]


def plus(own, got):
    return sum([x.astype(f32) for x in got], own.astype(f32))


def by_way(blocks):
    return (blocks[3], LINE, 1)


def rest_moves(blocks, passing):
    far = (blocks[2].astype(f32) + passing.astype(f32)).astype(bf16)
    return [(blocks[1], LINE, 1), (far, LINE, 2)]


def exchange(pieces, far_moves=(), far_beside=(), near_beside=()):
    got, near_beside = window([(pieces[k], "c", k) for k in range(1, pieces.shape[0])], near_beside)
    near = jnp.stack([pieces[0]] + got, axis=1)
    far_moves = far_moves(*near_beside) if callable(far_moves) else far_moves
    got, far_beside = window([(near[o], LINE, o) for o in range(1, 4)] + list(far_moves), far_beside)
    return [near[0]] + got[:3], got[3:], far_beside + near_beside


def in_place(got, me):
    whole = jnp.zeros((len(got),) + got[0].shape, got[0].dtype)
    for o, x in enumerate(got):
        whole = lax.dynamic_update_index_in_dim(whole, x, me ^ o, 0)
    return whole


def pick(x, i, axis=0):
    return lax.dynamic_index_in_dim(x, i, axis, keepdims=False)


def line_whole(got):
    return in_place(got, lax.axis_index(LINE))


def core_end(own, got):
    return jnp.moveaxis(in_place([own] + list(got), lax.axis_index("c")), 0, 1)


def core_share(parts, at):
    me = lax.axis_index("c")
    return [(pick(parts, me ^ o, at), "c", o) for o in range(1, lax.axis_size("c"))]


def core_sum(parts, got, at):
    return plus(pick(parts, lax.axis_index("c"), at), got).astype(bf16)


def line_blocks(near, at):
    return [pick(near, lax.axis_index(LINE) ^ o, at) for o in range(4)]


def positions(b, sub, cps, slot, dim, sb):
    shape = (sb, 1) if dim == 0 else (1, sb)
    lane = lax.broadcasted_iota(jnp.int32, shape, dim)
    return ((b ^ (sub * cps + lane // slot)) * slot) + lane % slot


def flip(x, factor=1.0):
    return jnp.transpose(x.astype(f32) * factor).astype(bf16)


def lifted(qrow, kcol):
    return dot(qrow, kcol, 1, 0) + 1.0


def repeat(lo, hi, step, value):
    if hi - lo <= 4:
        for i in range(lo, hi):
            value = step(i, value)
        return value
    return lax.fori_loop(lo, hi, step, value)


def fwd_kernel(nh, nb, slot, sb, ids, got0, got1, got2, got3, tiles, res, out, vrow, back):
    got, cores = (got0, got1, got2, got3), nb // 4
    nsub, cps = nb * slot // sb, sb // slot
    h, b = ids[0], ids[1]
    for o in range(nb):
        for oh in range(nh):
            at = (h ^ oh) * nsub + o // cps
            lo = (o % cps) * slot
            piece = got[o // cores][o % cores, :, oh * slot : (oh + 1) * slot]
            tiles[at, :, lo : lo + slot] = piece

    def rows_of(i, c):
        vv = jnp.concatenate([tiles[i, 32:144, :].astype(f32), jnp.ones((16, sb), f32)], axis=0)
        vrow[i] = jnp.transpose(vv).astype(bf16)
        return c

    repeat(0, nh * nsub, rows_of, 0)

    for hq in range(nh):
        for sub in range(nsub):
            iq = hq * nsub + sub
            qrow = flip(tiles[iq, 0:16, :], 0.25)
            pos_q = positions(b, sub, cps, slot, 0, sb)

            def step(ik, acc, masked):
                u = lifted(qrow, tiles[ik, 16:32, :])
                w = u * u + 1.0
                if masked:
                    pos_k = positions(b, ik - hq * nsub, cps, slot, 1, sb)
                    w = jnp.where(pos_q >= pos_k, w, 0.0)
                return acc + dot(w.astype(bf16), vrow[ik], 1, 0)

            acc = jnp.zeros((sb, 128), f32)
            acc = repeat(0, hq * nsub, functools.partial(step, masked=False), acc)
            acc = repeat(hq * nsub, (hq + 1) * nsub, functools.partial(step, masked=True), acc)
            den = acc[:, 112:113]
            mixed = acc / den
            lane = lax.broadcasted_iota(jnp.int32, (sb, 128), 1)
            res[iq] = jnp.where(lane == 112, den, mixed)
            back[iq] = jnp.transpose(mixed)[0:112].astype(bf16)
    for oh in range(nh):
        for o in range(nb):
            lo = (o % cps) * slot
            piece = back[(h ^ oh) * nsub + o // cps, :, lo : lo + slot]
            out[o % cores, o // cores, :, oh * slot : (oh + 1) * slot] = piece


def bwd_kernel(nh, nb, slot, sb, ids, tiles, res, got0, got1, got2, got3, out, gt, krow, acc):
    got, cores = (got0, got1, got2, got3), nb // 4
    nsub, cps = nb * slot // sb, sb // slot
    h, b = ids[0], ids[1]
    for o in range(nb):
        for oh in range(nh):
            at = (h ^ oh) * nsub + o // cps
            lo = (o % cps) * slot
            piece = got[o // cores][o % cores, :, oh * slot : (oh + 1) * slot]
            gt[at, :, lo : lo + slot] = piece

    def rows_of(i, c):
        krow[i] = flip(tiles[i, 16:32, :])
        acc[i] = jnp.zeros((144, sb), f32)
        return c

    repeat(0, nh * nsub, rows_of, 0)

    for hq in range(nh):
        for sub in range(nsub):
            iq = hq * nsub + sub
            qcol = tiles[iq, 0:16, :]
            qrow = flip(qcol, 0.25)
            gcol = gt[iq]
            grow = jnp.transpose(gcol.astype(f32))
            kept = res[iq]
            rden = 1.0 / kept[:, 112:113]
            rquarter = rden * 0.5
            delta = jnp.sum(grow * kept[:, 0:112], axis=1, keepdims=True)
            grow = grow.astype(bf16)
            pos_q = positions(b, sub, cps, slot, 0, sb)

            def step(ik, dq, masked):
                u = lifted(qrow, tiles[ik, 16:32, :])
                p = (u * u + 1.0) * rden
                ds = (dot(grow, tiles[ik, 32:144, :], 1, 0) - delta) * rquarter * u
                if masked:
                    pos_k = positions(b, ik - hq * nsub, cps, slot, 1, sb)
                    keep = pos_q >= pos_k
                    p = jnp.where(keep, p, 0.0)
                    ds = jnp.where(keep, ds, 0.0)
                p, ds = p.astype(bf16), ds.astype(bf16)
                acc[ik, 32:144, :] += dot(gcol, p, 1, 0)
                acc[ik, 16:32, :] += dot(qcol, ds, 1, 0)
                return dq + dot(ds, krow[ik], 1, 0)

            dq = jnp.zeros((sb, 16), f32)
            dq = repeat(0, hq * nsub, functools.partial(step, masked=False), dq)
            dq = repeat(hq * nsub, (hq + 1) * nsub, functools.partial(step, masked=True), dq)
            acc[iq, 0:16, :] = jnp.transpose(dq)
    for oh in range(nh):
        for o in range(nb):
            at = (h ^ oh) * nsub + o // cps
            lo = (o % cps) * slot
            piece = acc[at, :, lo : lo + slot].astype(bf16)
            out[o % cores, o // cores, :, oh * slot : (oh + 1) * slot] = piece


def rows_of(refs, s):
    return jnp.concatenate([x[s] for x in refs], axis=0)


def to_peers(cores, copies, b, pieces, out):
    for o in range(4 * cores):
        out[o % cores, o // cores] = pieces[(b ^ o) // copies]


def from_peers(cores, copies, b, got, pieces):
    for o in range(4 * cores):
        pieces[o] = got[o // cores][o % cores]
    return lambda p: pieces[b ^ (p * copies)]


def qkv_kernel(hd, copies, fw, vw, ids, x0, x1, x2, x3, w, out, pieces):
    cores = out.shape[0]
    for s in range(x0.shape[0]):
        rows = jnp.dot(rows_of((x0, x1, x2, x3), s), w[...], preferred_element_type=f32)
        cols = jnp.transpose(rows)
        for j in range(hd):
            at = (j * fw, (hd + j) * fw, 2 * hd * fw + j * vw)
            piece = [cols[lo : lo + n] for lo, n in zip(at, (fw, fw, vw))]
            pieces[s * hd + j] = jnp.concatenate(piece, axis=0).astype(bf16)
    to_peers(cores, copies, ids[1], pieces, out)


def out_kernel(hd, copies, ids, g0, g1, g2, g3, w, mixed, own, send, pieces):
    cores, vw, lanes = g0.shape
    seqs, slot = own.shape[:2]
    take = from_peers(cores, copies, ids[1], (g0, g1, g2, g3), pieces)
    for s in range(seqs):
        cols = jnp.concatenate([take(s * hd + j) for j in range(hd)], axis=0)
        mixed[:, s * lanes : (s + 1) * lanes] = cols
        rows = jnp.transpose(cols.astype(f32)).astype(bf16)
        part = jnp.dot(rows, w[...], preferred_element_type=f32)
        own[s] = part[:slot]
        for o in range(1, 4):
            send[o - 1, s] = part[o * slot : (o + 1) * slot].astype(bf16)


def mixed_back_kernel(hd, copies, ids, x0, x1, x2, x3, w, mixed, out, grad, pieces):
    cores, vw, lanes = out.shape[0], out.shape[2], out.shape[3]
    z, c = ids[2], ids[1] % cores
    rows = [rows_of((x0, x1, x2, x3), s) for s in range(x0.shape[0])]
    for s, x in enumerate(rows):
        cols = dot(w[...], x, 1, 1)
        for j in range(hd):
            pieces[s * hd + j] = cols[j * vw : (j + 1) * vw].astype(bf16)
    to_peers(cores, copies, ids[1], pieces, out)
    total = jnp.dot(mixed[...], jnp.concatenate(rows, axis=0), preferred_element_type=f32)
    drow = grad.shape[2]
    for k in range(4 * cores):
        grad[(k % cores) ^ c, (k // cores) ^ z] = total[k * drow : (k + 1) * drow].astype(bf16)


def qkv_back_kernel(
    hd, copies, fw, vw, ids, g0, g1, g2, g3, x0, x1, x2, x3, w, grad, own, send, pieces, cols
):
    cores, pw, lanes = g0.shape
    seqs, slot = own.shape[:2]
    z, c = ids[2], ids[1] % cores
    take = from_peers(cores, copies, ids[1], (g0, g1, g2, g3), pieces)
    for s in range(seqs):
        for j in range(hd):
            piece = take(s * hd + j)
            at = (j * fw, (hd + j) * fw, 2 * hd * fw + j * vw)
            lo = 0
            for row, n in zip(at, (fw, fw, vw)):
                cols[row : row + n, s * lanes : (s + 1) * lanes] = piece[lo : lo + n]
                lo += n
    rows = jnp.transpose(cols[...].astype(f32)).astype(bf16)
    for s in range(seqs):
        part = dot(rows[s * lanes : (s + 1) * lanes], w[...], 1, 1)
        own[s] = part[:slot]
        for o in range(1, 4):
            send[o - 1, s] = part[o * slot : (o + 1) * slot].astype(bf16)
    x = jnp.concatenate([rows_of((x0, x1, x2, x3), s) for s in range(seqs)], axis=0)
    drow, half = grad.shape[3], x.shape[1] // 2
    for i in range(2):
        total = dot(x[:, i * half : (i + 1) * half], rows, 0, 0)
        for k in range(half // drow):
            at = i * (half // drow) + k
            block = total[k * drow : (k + 1) * drow].astype(bf16)
            grad[(at % cores) ^ c, (at // cores % 4) ^ z, at // (4 * cores)] = block


def cut_kernel(nh, run, ids, gate, up, wq, wk, wv, out, heads):
    h, z = ids[0], ids[2]
    qw, vw = wq.shape[1] // nh, wv.shape[1] // nh
    for k in range(nh):
        parts = [wq[:, k * qw : (k + 1) * qw], wk[:, k * qw : (k + 1) * qw]]
        parts.append(wv[:, k * vw : (k + 1) * vw])
        heads[k ^ h] = jnp.concatenate([x.astype(f32) for x in parts], axis=1).astype(bf16)
    for zz in range(4):
        parts = []
        for w in (gate, up):
            parts += [w[:, (k * 4 + zz) * run : (k * 4 + zz + 1) * run] for k in range(nh)]
        out[zz ^ z] = jnp.concatenate([x.astype(f32) for x in parts], axis=1).astype(bf16)


def feed_kernel(nh, run, ids, p0, p1, p2, p3, gate, up, grad_gate, grad_up, total, pieces):
    z = ids[2]
    pieces[0], pieces[1], pieces[2], pieces[3] = p0[...], p1[...], p2[...], p3[...]
    for zz in range(4):
        piece = pieces[zz ^ z].astype(f32)
        for at, grad in ((0, grad_gate), (nh * run, grad_up)):
            for k in range(nh):
                lo = (k * 4 + zz) * run
                grad[:, lo : lo + run] = piece[:, at + k * run : at + (k + 1) * run]
    both = grad_gate[...] * gate[...].astype(f32) + grad_up[...] * up[...].astype(f32)
    total[...] = jnp.sum(both, axis=1, keepdims=True)


def heads_kernel(nh, qw, vw, ids, p0, p1, p2, p3, wq, wk, wv, gq, gk, gv, total, pieces):
    h = ids[0]
    pieces[0], pieces[1], pieces[2], pieces[3] = p0[...], p1[...], p2[...], p3[...]
    for k in range(nh):
        piece = pieces[k ^ h].astype(f32)
        gq[:, k * qw : (k + 1) * qw] = piece[:, :qw]
        gk[:, k * qw : (k + 1) * qw] = piece[:, qw : 2 * qw]
        gv[:, k * vw : (k + 1) * vw] = piece[:, 2 * qw :]
    sums = [
        jnp.sum(g[...] * w[...].astype(f32), axis=1, keepdims=True)
        for g, w in ((gq, wq), (gk, wk), (gv, wv))
    ]
    total[...] = sums[0] + sums[1] + sums[2]


def call(body, ids, arrays, outs, scratch, room=12):
    vmem = pl.BlockSpec(memory_space=pltpu.VMEM)
    held = list(arrays) + jax.tree.leaves(outs) + list(scratch)
    held = sum(math.prod(x.shape[:-1]) * max(x.shape[-1], 128) * x.dtype.itemsize for x in held)
    return pl.pallas_call(
        body,
        out_shape=outs,
        in_specs=[pl.BlockSpec(memory_space=pltpu.SMEM)] + [vmem] * len(arrays),
        out_specs=jax.tree.map(lambda _: vmem, outs),
        scratch_shapes=scratch,
        compiler_params=pltpu.CompilerParams(vmem_limit_bytes=held + room * 1024 * 1024),
    )(ids, *arrays)


def shards(
    tokens,
    cotangent,
    teacher,
    lengths,
    gain_attn,
    gain_mlp,
    w_query,
    w_key,
    w_value,
    w_out,
    w_gate,
    w_up,
    w_down,
):
    seqs, slot, width = tokens.shape
    cores = lax.axis_size("c")
    nh, nb = lax.axis_size(HEAD), 4 * cores
    h, b = lax.axis_index(HEAD), lax.axis_index(BLK)
    hd = H // nh
    pairs = seqs * hd
    copies = nb // pairs
    drow = w_query.shape[0]
    fw, vw = w_query.shape[1] // H, w_value.shape[1] // H
    pw = 2 * fw + vw
    ffl = w_gate.shape[1] // 4
    lanes = nh * slot
    sb = min(512, nb * slot)
    n = nb * slot * nh // sb
    ids = jnp.stack([h, b, lax.axis_index(LINE)]).astype(jnp.int32)

    def gathered(x):
        return lax.all_gather(x[None], CROSS, axis=0, tiled=True)

    def summed(shares):
        return lax.psum_scatter(shares, CROSS, scatter_dimension=0)

    run = w_gate.shape[1] // (4 * nh)
    ffn_cols, qkv_cols = call(
        functools.partial(cut_kernel, nh, run),
        ids,
        [w_gate, w_up, w_query, w_key, w_value],
        [
            jax.ShapeDtypeStruct((4, drow, 2 * ffl), bf16),
            jax.ShapeDtypeStruct((nh, drow, hd * pw), bf16),
        ],
        [],
    )

    place = (h * nb + b) * slot + lax.broadcasted_iota(jnp.int32, (seqs, slot), 1)
    valid = (place < lengths[:, None]).astype(f32)[..., None]
    count = jnp.sum(lengths).astype(f32)

    tokens_f = tokens.astype(f32)
    scale_one = rms_scale(tokens_f)
    own_rows = (tokens_f * scale_one * gain_attn).astype(bf16)
    (*got, ffn_1, ffn_2), (own_rows,) = window(
        return_moves(qkv_cols, HEAD) + [(ffn_cols[1], LINE, 1), (ffn_cols[2], LINE, 2)], (own_rows,)
    )
    qkv_cols = in_place([qkv_cols[0]] + got, h)
    (row_1, row_2, qkv_near, qkv_far), _ = window(
        [(own_rows, HEAD, 1), (own_rows, HEAD, 2), (qkv_cols, LINE, 1), (qkv_cols, LINE, 2)]
    )
    (row_3, qkv_last, ffn_3), _ = window(
        [(own_rows, HEAD, 3), (qkv_far, LINE, 1), (ffn_cols[3], LINE, 3)]
    )
    attn_rows = [own_rows, row_1, row_2, row_3]
    qkv_w = line_whole([qkv_cols, qkv_near, qkv_far, qkv_last])
    got, (ffn_cols,) = window(
        over(qkv_w, "c"), (line_whole([ffn_cols[0], ffn_1, ffn_2, ffn_3]),)
    )
    ffn_w = gathered(ffn_cols)
    ffn_w = ffn_w.reshape(nh, cores, 4, drow, -1).transpose(0, 2, 1, 3, 4).reshape(width, -1)
    qkv_w = core_end(qkv_w, got).transpose(2, 0, 1, 3, 4).reshape(width, -1)
    geometry = (nh, nb, slot, sb)
    piece = lambda rows: jax.ShapeDtypeStruct((cores, 4, rows, lanes), bf16)
    held = lambda rows: [pltpu.VMEM((pairs, rows, lanes), bf16)]
    taken = lambda rows: [pltpu.VMEM((nb, rows, lanes), bf16)]
    own_part = jax.ShapeDtypeStruct((seqs, slot, width), f32)
    sent_part = jax.ShapeDtypeStruct((3, seqs, slot, width), bf16)
    pieces = call(
        functools.partial(qkv_kernel, hd, copies, fw, vw),
        ids,
        attn_rows + [qkv_w],
        piece(pw),
        held(pw),
        room=36,
    )
    sent, _, (down_w, w_out_late) = exchange(pieces, far_beside=(gathered(w_down), w_out))
    down_w = down_w.reshape(-1, width)
    out_near, out_far = swap(w_out_late, LINE, 1), swap(w_out_late, LINE, 2)
    tiles, res, mixed_out = call(
        functools.partial(fwd_kernel, *geometry),
        ids,
        sent,
        [
            jax.ShapeDtypeStruct((n, pw, sb), bf16),
            jax.ShapeDtypeStruct((n, sb, 128), f32),
            piece(vw),
        ],
        [pltpu.VMEM((n, sb, 128), bf16), pltpu.VMEM((n, vw, sb), bf16)],
        room=36,
    )
    mixed_got, (out_last,), (out_near, out_far) = exchange(
        mixed_out,
        far_moves=lambda near, far: [(far, LINE, 1)],
        near_beside=(out_near, out_far),
    )
    out_w = line_whole([w_out, out_near, out_far, out_last])
    got, (out_w,) = window(over(out_w, "c"), (out_w,))
    out_w = core_end(out_w, got).reshape(-1, width)
    mixed, attn_own, attn_part = call(
        functools.partial(out_kernel, hd, copies),
        ids,
        mixed_got + [out_w],
        [jax.ShapeDtypeStruct((hd * vw, seqs * lanes), bf16), own_part, sent_part],
        taken(vw),
        room=36,
    )
    got, (ffn_w,) = window([(attn_part[o - 1], HEAD, o) for o in range(1, 4)], (ffn_w,))
    residual = tokens_f + plus(attn_own, got)

    scale_two = rms_scale(residual)
    own_rows = (residual * scale_two * gain_mlp).astype(bf16)

    def forward(*rows):
        both = dot(jnp.concatenate([x.reshape(-1, width) for x in rows]), ffn_w, 1, 0)
        gate, up = both[:, :ffl], both[:, ffl:]
        hidden = (jax.nn.silu(gate) * up).astype(bf16)
        part = dot(hidden, down_w, 1, 0).reshape(len(rows), seqs, slot, width)
        return gate, up, hidden, part

    (near, far), first = window([(own_rows, LINE, 1), (own_rows, LINE, 2)], forward(own_rows))
    (last,), second = window([(far, LINE, 1)], forward(near, far))
    kept = [first, second, forward(last)]
    part = [y for x in kept for y in x[3]]
    normed_mlp = jnp.concatenate([x.reshape(-1, width) for x in (own_rows, near, far, last)])
    hidden = jnp.concatenate([x[2] for x in kept])
    passing = swap(part[3].astype(bf16), LINE, 1)
    got, _ = window(rest_moves([x.astype(bf16) for x in part], passing))
    full = valid * (residual + plus(part[0], got))
    diff = full - teacher.astype(f32)
    (loss,) = tie(jnp.full((1, 64, 128), jnp.sum(valid * diff * diff)))
    loss = lax.all_gather(loss, AXES, axis=0, tiled=True)

    grad_res = valid * (cotangent.astype(f32) + 2.0 * valid * diff / (width * count))
    own_rows = grad_res.astype(bf16)

    def backward(rows, gate, up):
        grad_hidden = dot(jnp.concatenate([x.reshape(-1, width) for x in rows]), down_w, 1, 1)
        sigma = jax.nn.sigmoid(gate)
        slope = sigma * (1.0 + gate * (1.0 - sigma))
        grad_gate = (grad_hidden * up * slope).astype(bf16)
        grad_up = (grad_hidden * gate * sigma).astype(bf16)
        grad_both = jnp.concatenate([grad_gate, grad_up], axis=1)
        return grad_both, dot(grad_both, ffn_w, 1, 1).reshape(len(rows), seqs, slot, width)

    def norm_back(grad_norm, values, scale_rows, gain):
        unit = values * scale_rows
        e = grad_norm * gain
        return scale_rows * (e - unit * jnp.mean(e * unit, axis=-1, keepdims=True))

    (near, far), first = window(
        [(own_rows, LINE, 1), (own_rows, LINE, 2)], backward((own_rows,), *kept[0][:2])
    )
    (last,), second = window([(far, LINE, 1)], backward((near, far), *kept[1][:2]))
    back = [first, second, backward((last,), *kept[2][:2])]
    part = [y for x in back for y in x[1]]
    passing = swap(part[3].astype(bf16), LINE, 1)
    grad_both = jnp.concatenate([x[0] for x in back])
    grad_ffn = jnp.concatenate([x.reshape(-1, width) for x in (own_rows, near, far, last)])
    part, grad_both, hidden = tie(part, grad_both, hidden)
    grad_down = dot(hidden, grad_ffn, 0, 0).astype(bf16).reshape(nb, -1, width)
    passing, grad_down, normed_mlp = tie(passing, grad_down, normed_mlp)
    grad_down = summed(grad_down)
    grad_ffn_w = dot(normed_mlp, grad_both, 0, 0).astype(bf16)
    grad_ffn_w = grad_ffn_w.reshape(nh, 4, cores, drow, -1).transpose(0, 2, 1, 3, 4)
    shares = grad_ffn_w.reshape(nb, 4 * drow, -1)
    got, (shares, loss) = window(rest_moves([x.astype(bf16) for x in part], passing), (shares, loss))
    grad_ffn_w = summed(shares)
    loss = jnp.sum(loss[:, 0, 0]) / (width * count)
    grad_resid = grad_res + norm_back(plus(part[0], got), residual, scale_two, gain_mlp)
    own_rows = grad_resid.astype(bf16)
    got, _ = window(over(own_rows, HEAD))
    sent, grad_out_w = call(
        functools.partial(mixed_back_kernel, hd, copies),
        ids,
        [own_rows] + got + [out_w, mixed],
        [piece(vw), jax.ShapeDtypeStruct((cores, 4, drow, width), bf16)],
        held(vw),
        room=36,
    )
    sent, out_got, _ = exchange(
        sent, far_moves=[(grad_out_w[k], "c", k) for k in range(1, cores)]
    )
    grad_out_w = plus(grad_out_w[0], out_got).astype(bf16)
    sent, grad_out_w = tie(sent, grad_out_w)
    out_got = [swap(grad_out_w[o], LINE, o) for o in range(1, 3)]
    grads_out = call(
        functools.partial(bwd_kernel, *geometry),
        ids,
        [tiles, res] + sent,
        piece(pw),
        [
            pltpu.VMEM((n, vw, sb), bf16),
            pltpu.VMEM((n, sb, fw), bf16),
            pltpu.VMEM((n, pw, sb), f32),
        ],
        room=36,
    )
    grads_out, out_got = tie(grads_out, out_got)
    grad_qkv, _, (grad_ffn_w,) = exchange(grads_out, far_beside=(grad_ffn_w,))
    grad_qkv_w, own_back, attn_back = call(
        functools.partial(qkv_back_kernel, hd, copies, fw, vw),
        ids,
        grad_qkv + attn_rows + [qkv_w],
        [jax.ShapeDtypeStruct((cores, 4, nh, drow, hd * pw), bf16), own_part, sent_part],
        taken(pw) + [pltpu.VMEM((hd * pw, seqs * lanes), bf16)],
        room=36,
    )
    grad_qkv_w, grad_ffn_w = tie(grad_qkv_w, grad_ffn_w)
    grad_ffn_w = grad_ffn_w.reshape(4, drow, -1)
    ffn_pieces = [pick(grad_ffn_w, lax.axis_index(LINE) ^ o) for o in range(4)]
    row_moves = [(attn_back[o - 1], HEAD, o) for o in range(1, 4)]
    got, _ = window([(grad_qkv_w[k], "c", k) for k in range(1, cores)])
    grad_qkv_w = plus(grad_qkv_w[0], got).astype(bf16)
    (passing, ffn_2, out_last, *row_got), _ = window(
        [by_way(grad_qkv_w), (ffn_pieces[2], LINE, 2), (grad_out_w[3], LINE, 3)] + row_moves[:2]
    )
    out_got = out_got + [out_last]
    (got_1, got_2, last, ffn_1), _ = window(
        rest_moves(grad_qkv_w, passing) + [row_moves[2], (ffn_pieces[1], LINE, 1)]
    )
    row_got = row_got + [last]
    grad_qkv_w = plus(grad_qkv_w[0], [got_1, got_2]).astype(bf16)
    (*got, ffn_3), _ = window(turn_moves(grad_qkv_w, HEAD) + [(ffn_pieces[3], LINE, 3)])
    grad_down, got = tie(grad_down, got)
    rows_f32 = lambda w: jax.ShapeDtypeStruct(w.shape, f32)
    one = jax.ShapeDtypeStruct((drow, 1), f32)
    gg, gu, gain_sum_two = call(
        functools.partial(feed_kernel, nh, run),
        ids,
        [ffn_pieces[0], ffn_1, ffn_2, ffn_3, w_gate, w_up],
        [rows_f32(w_gate), rows_f32(w_up), one],
        [pltpu.VMEM((4, drow, 2 * ffl), bf16)],
    )
    gq, gk, gv, gain_sum_one = call(
        functools.partial(heads_kernel, nh, hd * fw, hd * vw),
        ids,
        [pick(grad_qkv_w, h)] + got + [w_query, w_key, w_value],
        [rows_f32(w_query), rows_f32(w_key), rows_f32(w_value), one],
        [pltpu.VMEM((4, drow, hd * pw), bf16)],
    )
    grad_out_w = plus(grad_out_w[0], out_got)
    grad_in = plus(own_back, row_got)
    grad_tokens = grad_resid + norm_back(grad_in, tokens_f, scale_one, gain_attn)

    def gain_grad(total, gain):
        at = lax.axis_index(AXES) * drow
        return total[:, 0] / lax.dynamic_slice(gain, (at,), (drow,))

    return (
        full.astype(bf16),
        loss,
        grad_tokens,
        gq,
        gk,
        gv,
        grad_out_w.astype(f32),
        gg,
        gu,
        grad_down.astype(f32),
        gain_grad(gain_sum_one, gain_attn),
        gain_grad(gain_sum_two, gain_mlp),
    )


def solution(mesh):
    parts = Mesh(mesh.devices.reshape(mesh.shape["head"], 4, -1), AXES)
    rows, slots = P(AXES, None), P(None, AXES, None)
    return jax.shard_map(
        shards,
        mesh=parts,
        in_specs=(slots,) * 3 + (P(),) * 3 + (rows,) * 7,
        out_specs=(slots, P(), slots) + (rows,) * 7 + (P(AXES),) * 2,
        check_vma=False,
    )
```

```python
import functools
import math

import jax
import jax.numpy as jnp
from jax import lax
from jax.experimental import pallas as pl
from jax.experimental.pallas import tpu as pltpu
from jax.sharding import Mesh
from jax.sharding import PartitionSpec as P

H = 16
norm_eps = 1e-06
bf16, f32 = jnp.bfloat16, jnp.float32


def dot(a, b, ca, cb):
    return lax.dot_general(a, b, (((ca,), (cb,)), ((), ())), preferred_element_type=f32)


def swap(x, axis, o):
    n = lax.axis_size(axis)
    return lax.ppermute(x, axis, [(i, i ^ o) for i in range(n)])


def rms_scale(values):
    return lax.rsqrt(jnp.mean(values * values, axis=-1, keepdims=True) + norm_eps)


HEAD, LINE, BLK, CROSS = "head", "z", ("z", "c"), ("head", "c")
AXES = (HEAD,) + BLK


def tie(*values):
    return lax.optimization_barrier(values)


def window(moves, beside=()):
    arrays = tie(*[x for x, _, _ in moves])
    return tie([swap(x, axis, o) for x, (_, axis, o) in zip(arrays, moves)], beside)


def over(x, axis):
    return [(x, axis, o) for o in range(1, lax.axis_size(axis))]


def turn_moves(pieces, axis):
    me = lax.axis_index(axis)
    return [(pick(pieces, me ^ o), axis, o) for o in range(1, lax.axis_size(axis))]


def turned(pieces, got, axis):
    me = lax.axis_index(axis)
    return in_place([pick(pieces, me)] + list(got), me)


def return_moves(parts, axis):
    return [(x, axis, o) for o, x in enumerate(parts) if o]


def plus(own, got):
    return sum([x.astype(f32) for x in got], own.astype(f32))


def by_way(blocks):
    return (blocks[3], LINE, 1)


def rest_moves(blocks, passing):
    far = (blocks[2].astype(f32) + passing.astype(f32)).astype(bf16)
    return [(blocks[1], LINE, 1), (far, LINE, 2)]


def exchange(pieces, far_moves=(), far_beside=(), near_beside=()):
    got, near_beside = window([(pieces[k], "c", k) for k in range(1, pieces.shape[0])], near_beside)
    near = jnp.stack([pieces[0]] + got, axis=1)
    far_moves = far_moves(*near_beside) if callable(far_moves) else far_moves
    got, far_beside = window([(near[o], LINE, o) for o in range(1, 4)] + list(far_moves), far_beside)
    return [near[0]] + got[:3], got[3:], far_beside + near_beside


def in_place(got, me):
    whole = jnp.zeros((len(got),) + got[0].shape, got[0].dtype)
    for o, x in enumerate(got):
        whole = lax.dynamic_update_index_in_dim(whole, x, me ^ o, 0)
    return whole


def pick(x, i, axis=0):
    return lax.dynamic_index_in_dim(x, i, axis, keepdims=False)


def line_whole(got):
    return in_place(got, lax.axis_index(LINE))


def core_end(own, got):
    return jnp.moveaxis(in_place([own] + list(got), lax.axis_index("c")), 0, 1)


def core_share(parts, at):
    me = lax.axis_index("c")
    return [(pick(parts, me ^ o, at), "c", o) for o in range(1, lax.axis_size("c"))]


def core_sum(parts, got, at):
    return plus(pick(parts, lax.axis_index("c"), at), got).astype(bf16)


def line_blocks(near, at):
    return [pick(near, lax.axis_index(LINE) ^ o, at) for o in range(4)]


def positions(b, sub, cps, slot, dim, sb):
    shape = (sb, 1) if dim == 0 else (1, sb)
    lane = lax.broadcasted_iota(jnp.int32, shape, dim)
    return ((b ^ (sub * cps + lane // slot)) * slot) + lane % slot


def flip(x, factor=1.0):
    return jnp.transpose(x.astype(f32) * factor).astype(bf16)


def lifted(qrow, kcol):
    return dot(qrow, kcol, 1, 0) + 1.0


def repeat(lo, hi, step, value):
    if hi - lo <= 4:
        for i in range(lo, hi):
            value = step(i, value)
        return value
    return lax.fori_loop(lo, hi, step, value)


def fwd_kernel(nh, nb, slot, sb, ids, got0, got1, got2, got3, tiles, res, out, vrow, back):
    got, cores = (got0, got1, got2, got3), nb // 4
    nsub, cps = nb * slot // sb, sb // slot
    h, b = ids[0], ids[1]
    for o in range(nb):
        for oh in range(nh):
            at = (h ^ oh) * nsub + o // cps
            lo = (o % cps) * slot
            piece = got[o // cores][o % cores, :, oh * slot : (oh + 1) * slot]
            tiles[at, :, lo : lo + slot] = piece

    def rows_of(i, c):
        vv = jnp.concatenate([tiles[i, 32:144, :].astype(f32), jnp.ones((16, sb), f32)], axis=0)
        vrow[i] = jnp.transpose(vv).astype(bf16)
        return c

    repeat(0, nh * nsub, rows_of, 0)

    for hq in range(nh):
        for sub in range(nsub):
            iq = hq * nsub + sub
            qrow = flip(tiles[iq, 0:16, :], 0.25)
            pos_q = positions(b, sub, cps, slot, 0, sb)

            def step(ik, acc, masked):
                u = lifted(qrow, tiles[ik, 16:32, :])
                w = u * u + 1.0
                if masked:
                    pos_k = positions(b, ik - hq * nsub, cps, slot, 1, sb)
                    w = jnp.where(pos_q >= pos_k, w, 0.0)
                return acc + dot(w.astype(bf16), vrow[ik], 1, 0)

            acc = jnp.zeros((sb, 128), f32)
            acc = repeat(0, hq * nsub, functools.partial(step, masked=False), acc)
            acc = repeat(hq * nsub, (hq + 1) * nsub, functools.partial(step, masked=True), acc)
            den = acc[:, 112:113]
            mixed = acc / den
            lane = lax.broadcasted_iota(jnp.int32, (sb, 128), 1)
            res[iq] = jnp.where(lane == 112, den, mixed)
            back[iq] = jnp.transpose(mixed)[0:112].astype(bf16)
    for oh in range(nh):
        for o in range(nb):
            lo = (o % cps) * slot
            piece = back[(h ^ oh) * nsub + o // cps, :, lo : lo + slot]
            out[o % cores, o // cores, :, oh * slot : (oh + 1) * slot] = piece


def bwd_kernel(nh, nb, slot, sb, ids, tiles, res, got0, got1, got2, got3, out, gt, krow, acc):
    got, cores = (got0, got1, got2, got3), nb // 4
    nsub, cps = nb * slot // sb, sb // slot
    h, b = ids[0], ids[1]
    for o in range(nb):
        for oh in range(nh):
            at = (h ^ oh) * nsub + o // cps
            lo = (o % cps) * slot
            piece = got[o // cores][o % cores, :, oh * slot : (oh + 1) * slot]
            gt[at, :, lo : lo + slot] = piece

    def rows_of(i, c):
        krow[i] = flip(tiles[i, 16:32, :])
        acc[i] = jnp.zeros((144, sb), f32)
        return c

    repeat(0, nh * nsub, rows_of, 0)

    for hq in range(nh):
        for sub in range(nsub):
            iq = hq * nsub + sub
            qcol = tiles[iq, 0:16, :]
            qrow = flip(qcol, 0.25)
            gcol = gt[iq]
            grow = jnp.transpose(gcol.astype(f32))
            kept = res[iq]
            rden = 1.0 / kept[:, 112:113]
            rquarter = rden * 0.5
            delta = jnp.sum(grow * kept[:, 0:112], axis=1, keepdims=True)
            grow = grow.astype(bf16)
            pos_q = positions(b, sub, cps, slot, 0, sb)

            def step(ik, dq, masked):
                u = lifted(qrow, tiles[ik, 16:32, :])
                p = (u * u + 1.0) * rden
                ds = (dot(grow, tiles[ik, 32:144, :], 1, 0) - delta) * rquarter * u
                if masked:
                    pos_k = positions(b, ik - hq * nsub, cps, slot, 1, sb)
                    keep = pos_q >= pos_k
                    p = jnp.where(keep, p, 0.0)
                    ds = jnp.where(keep, ds, 0.0)
                p, ds = p.astype(bf16), ds.astype(bf16)
                acc[ik, 32:144, :] += dot(gcol, p, 1, 0)
                acc[ik, 16:32, :] += dot(qcol, ds, 1, 0)
                return dq + dot(ds, krow[ik], 1, 0)

            dq = jnp.zeros((sb, 16), f32)
            dq = repeat(0, hq * nsub, functools.partial(step, masked=False), dq)
            dq = repeat(hq * nsub, (hq + 1) * nsub, functools.partial(step, masked=True), dq)
            acc[iq, 0:16, :] = jnp.transpose(dq)
    for oh in range(nh):
        for o in range(nb):
            at = (h ^ oh) * nsub + o // cps
            lo = (o % cps) * slot
            piece = acc[at, :, lo : lo + slot].astype(bf16)
            out[o % cores, o // cores, :, oh * slot : (oh + 1) * slot] = piece


def rows_of(refs, s):
    return jnp.concatenate([x[s] for x in refs], axis=0)


def to_peers(cores, copies, b, pieces, out):
    for o in range(4 * cores):
        out[o % cores, o // cores] = pieces[(b ^ o) // copies]


def from_peers(cores, copies, b, got, pieces):
    for o in range(4 * cores):
        pieces[o] = got[o // cores][o % cores]
    return lambda p: pieces[b ^ (p * copies)]


def qkv_kernel(hd, copies, fw, vw, ids, x0, x1, x2, x3, w, out, pieces):
    cores = out.shape[0]
    for s in range(x0.shape[0]):
        rows = jnp.dot(rows_of((x0, x1, x2, x3), s), w[...], preferred_element_type=f32)
        cols = jnp.transpose(rows)
        for j in range(hd):
            at = (j * fw, (hd + j) * fw, 2 * hd * fw + j * vw)
            piece = [cols[lo : lo + n] for lo, n in zip(at, (fw, fw, vw))]
            pieces[s * hd + j] = jnp.concatenate(piece, axis=0).astype(bf16)
    to_peers(cores, copies, ids[1], pieces, out)


def out_kernel(hd, copies, ids, g0, g1, g2, g3, w, mixed, own, send, pieces):
    cores, vw, lanes = g0.shape
    seqs, slot = own.shape[:2]
    take = from_peers(cores, copies, ids[1], (g0, g1, g2, g3), pieces)
    for s in range(seqs):
        cols = jnp.concatenate([take(s * hd + j) for j in range(hd)], axis=0)
        mixed[:, s * lanes : (s + 1) * lanes] = cols
        rows = jnp.transpose(cols.astype(f32)).astype(bf16)
        part = jnp.dot(rows, w[...], preferred_element_type=f32)
        own[s] = part[:slot]
        for o in range(1, 4):
            send[o - 1, s] = part[o * slot : (o + 1) * slot].astype(bf16)


def mixed_back_kernel(hd, copies, ids, x0, x1, x2, x3, w, mixed, out, grad, pieces):
    cores, vw, lanes = out.shape[0], out.shape[2], out.shape[3]
    z, c = ids[2], ids[1] % cores
    rows = [rows_of((x0, x1, x2, x3), s) for s in range(x0.shape[0])]
    for s, x in enumerate(rows):
        cols = dot(w[...], x, 1, 1)
        for j in range(hd):
            pieces[s * hd + j] = cols[j * vw : (j + 1) * vw].astype(bf16)
    to_peers(cores, copies, ids[1], pieces, out)
    total = jnp.dot(mixed[...], jnp.concatenate(rows, axis=0), preferred_element_type=f32)
    drow = grad.shape[2]
    for k in range(4 * cores):
        grad[(k % cores) ^ c, (k // cores) ^ z] = total[k * drow : (k + 1) * drow].astype(bf16)


def qkv_back_kernel(
    hd, copies, fw, vw, ids, g0, g1, g2, g3, x0, x1, x2, x3, w, grad, own, send, pieces, cols
):
    cores, pw, lanes = g0.shape
    seqs, slot = own.shape[:2]
    z, c = ids[2], ids[1] % cores
    take = from_peers(cores, copies, ids[1], (g0, g1, g2, g3), pieces)
    for s in range(seqs):
        for j in range(hd):
            piece = take(s * hd + j)
            at = (j * fw, (hd + j) * fw, 2 * hd * fw + j * vw)
            lo = 0
            for row, n in zip(at, (fw, fw, vw)):
                cols[row : row + n, s * lanes : (s + 1) * lanes] = piece[lo : lo + n]
                lo += n
    rows = jnp.transpose(cols[...].astype(f32)).astype(bf16)
    for s in range(seqs):
        part = dot(rows[s * lanes : (s + 1) * lanes], w[...], 1, 1)
        own[s] = part[:slot]
        for o in range(1, 4):
            send[o - 1, s] = part[o * slot : (o + 1) * slot].astype(bf16)
    x = jnp.concatenate([rows_of((x0, x1, x2, x3), s) for s in range(seqs)], axis=0)
    drow, half = grad.shape[3], x.shape[1] // 2
    for i in range(2):
        total = dot(x[:, i * half : (i + 1) * half], rows, 0, 0)
        for k in range(half // drow):
            at = i * (half // drow) + k
            block = total[k * drow : (k + 1) * drow].astype(bf16)
            grad[(at % cores) ^ c, (at // cores % 4) ^ z, at // (4 * cores)] = block


def cut_kernel(nh, run, ids, gate, up, wq, wk, wv, out, heads):
    h, z = ids[0], ids[2]
    qw, vw = wq.shape[1] // nh, wv.shape[1] // nh
    for k in range(nh):
        parts = [wq[:, k * qw : (k + 1) * qw], wk[:, k * qw : (k + 1) * qw]]
        parts.append(wv[:, k * vw : (k + 1) * vw])
        heads[k ^ h] = jnp.concatenate([x.astype(f32) for x in parts], axis=1).astype(bf16)
    for zz in range(4):
        parts = []
        for w in (gate, up):
            parts += [w[:, (k * 4 + zz) * run : (k * 4 + zz + 1) * run] for k in range(nh)]
        out[zz ^ z] = jnp.concatenate([x.astype(f32) for x in parts], axis=1).astype(bf16)


def feed_kernel(nh, run, ids, p0, p1, p2, p3, gate, up, grad_gate, grad_up, total, pieces):
    z = ids[2]
    pieces[0], pieces[1], pieces[2], pieces[3] = p0[...], p1[...], p2[...], p3[...]
    for zz in range(4):
        piece = pieces[zz ^ z].astype(f32)
        for at, grad in ((0, grad_gate), (nh * run, grad_up)):
            for k in range(nh):
                lo = (k * 4 + zz) * run
                grad[:, lo : lo + run] = piece[:, at + k * run : at + (k + 1) * run]
    both = grad_gate[...] * gate[...].astype(f32) + grad_up[...] * up[...].astype(f32)
    total[...] = jnp.sum(both, axis=1, keepdims=True)


def heads_kernel(nh, qw, vw, ids, p0, p1, p2, p3, wq, wk, wv, gq, gk, gv, total, pieces):
    h = ids[0]
    pieces[0], pieces[1], pieces[2], pieces[3] = p0[...], p1[...], p2[...], p3[...]
    for k in range(nh):
        piece = pieces[k ^ h].astype(f32)
        gq[:, k * qw : (k + 1) * qw] = piece[:, :qw]
        gk[:, k * qw : (k + 1) * qw] = piece[:, qw : 2 * qw]
        gv[:, k * vw : (k + 1) * vw] = piece[:, 2 * qw :]
    sums = [
        jnp.sum(g[...] * w[...].astype(f32), axis=1, keepdims=True)
        for g, w in ((gq, wq), (gk, wk), (gv, wv))
    ]
    total[...] = sums[0] + sums[1] + sums[2]


def call(body, ids, arrays, outs, scratch, room=12):
    vmem = pl.BlockSpec(memory_space=pltpu.VMEM)
    held = list(arrays) + jax.tree.leaves(outs) + list(scratch)
    held = sum(math.prod(x.shape[:-1]) * max(x.shape[-1], 128) * x.dtype.itemsize for x in held)
    return pl.pallas_call(
        body,
        out_shape=outs,
        in_specs=[pl.BlockSpec(memory_space=pltpu.SMEM)] + [vmem] * len(arrays),
        out_specs=jax.tree.map(lambda _: vmem, outs),
        scratch_shapes=scratch,
        compiler_params=pltpu.CompilerParams(vmem_limit_bytes=held + room * 1024 * 1024),
    )(ids, *arrays)


def shards(
    tokens,
    cotangent,
    teacher,
    lengths,
    gain_attn,
    gain_mlp,
    w_query,
    w_key,
    w_value,
    w_out,
    w_gate,
    w_up,
    w_down,
):
    seqs, slot, width = tokens.shape
    cores = lax.axis_size("c")
    nh, nb = lax.axis_size(HEAD), 4 * cores
    h, b = lax.axis_index(HEAD), lax.axis_index(BLK)
    hd = H // nh
    pairs = seqs * hd
    copies = nb // pairs
    drow = w_query.shape[0]
    fw, vw = w_query.shape[1] // H, w_value.shape[1] // H
    pw = 2 * fw + vw
    ffl = w_gate.shape[1] // 4
    lanes = nh * slot
    sb = min(512, nb * slot)
    n = nb * slot * nh // sb
    ids = jnp.stack([h, b, lax.axis_index(LINE)]).astype(jnp.int32)

    def gathered(x):
        return lax.all_gather(x[None], CROSS, axis=0, tiled=True)

    def summed(shares):
        return lax.psum_scatter(shares, CROSS, scatter_dimension=0)

    run = w_gate.shape[1] // (4 * nh)
    ffn_cols, qkv_cols = call(
        functools.partial(cut_kernel, nh, run),
        ids,
        [w_gate, w_up, w_query, w_key, w_value],
        [
            jax.ShapeDtypeStruct((4, drow, 2 * ffl), bf16),
            jax.ShapeDtypeStruct((nh, drow, hd * pw), bf16),
        ],
        [],
    )

    place = (h * nb + b) * slot + lax.broadcasted_iota(jnp.int32, (seqs, slot), 1)
    valid = (place < lengths[:, None]).astype(f32)[..., None]
    count = jnp.sum(lengths).astype(f32)

    tokens_f = tokens.astype(f32)
    scale_one = rms_scale(tokens_f)
    own_rows = (tokens_f * scale_one * gain_attn).astype(bf16)
    (*got, ffn_1, ffn_2), (own_rows,) = window(
        return_moves(qkv_cols, HEAD) + [(ffn_cols[1], LINE, 1), (ffn_cols[2], LINE, 2)], (own_rows,)
    )
    qkv_cols = in_place([qkv_cols[0]] + got, h)
    (row_1, row_2, qkv_near, qkv_far), _ = window(
        [(own_rows, HEAD, 1), (own_rows, HEAD, 2), (qkv_cols, LINE, 1), (qkv_cols, LINE, 2)]
    )
    (row_3, qkv_last, ffn_3), _ = window(
        [(own_rows, HEAD, 3), (qkv_far, LINE, 1), (ffn_cols[3], LINE, 3)]
    )
    attn_rows = [own_rows, row_1, row_2, row_3]
    qkv_w = line_whole([qkv_cols, qkv_near, qkv_far, qkv_last])
    got, (ffn_cols,) = window(
        over(qkv_w, "c"), (line_whole([ffn_cols[0], ffn_1, ffn_2, ffn_3]),)
    )
    ffn_w = gathered(ffn_cols)
    ffn_w = ffn_w.reshape(nh, cores, 4, drow, -1).transpose(0, 2, 1, 3, 4).reshape(width, -1)
    qkv_w = core_end(qkv_w, got).transpose(2, 0, 1, 3, 4).reshape(width, -1)
    geometry = (nh, nb, slot, sb)
    piece = lambda rows: jax.ShapeDtypeStruct((cores, 4, rows, lanes), bf16)
    held = lambda rows: [pltpu.VMEM((pairs, rows, lanes), bf16)]
    taken = lambda rows: [pltpu.VMEM((nb, rows, lanes), bf16)]
    own_part = jax.ShapeDtypeStruct((seqs, slot, width), f32)
    sent_part = jax.ShapeDtypeStruct((3, seqs, slot, width), bf16)
    pieces = call(
        functools.partial(qkv_kernel, hd, copies, fw, vw),
        ids,
        attn_rows + [qkv_w],
        piece(pw),
        held(pw),
        room=36,
    )
    sent, _, (down_w, w_out_late) = exchange(pieces, far_beside=(gathered(w_down), w_out))
    down_w = down_w.reshape(-1, width)
    out_near, out_far = swap(w_out_late, LINE, 1), swap(w_out_late, LINE, 2)
    tiles, res, mixed_out = call(
        functools.partial(fwd_kernel, *geometry),
        ids,
        sent,
        [
            jax.ShapeDtypeStruct((n, pw, sb), bf16),
            jax.ShapeDtypeStruct((n, sb, 128), f32),
            piece(vw),
        ],
        [pltpu.VMEM((n, sb, 128), bf16), pltpu.VMEM((n, vw, sb), bf16)],
        room=36,
    )
    mixed_got, (out_last,), (out_near, out_far) = exchange(
        mixed_out,
        far_moves=lambda near, far: [(far, LINE, 1)],
        near_beside=(out_near, out_far),
    )
    out_w = line_whole([w_out, out_near, out_far, out_last])
    got, (out_w,) = window(over(out_w, "c"), (out_w,))
    out_w = core_end(out_w, got).reshape(-1, width)
    mixed, attn_own, attn_part = call(
        functools.partial(out_kernel, hd, copies),
        ids,
        mixed_got + [out_w],
        [jax.ShapeDtypeStruct((hd * vw, seqs * lanes), bf16), own_part, sent_part],
        taken(vw),
        room=36,
    )
    got, (ffn_w,) = window([(attn_part[o - 1], HEAD, o) for o in range(1, 4)], (ffn_w,))
    residual = tokens_f + plus(attn_own, got)

    scale_two = rms_scale(residual)
    own_rows = (residual * scale_two * gain_mlp).astype(bf16)

    def forward(*rows):
        both = dot(jnp.concatenate([x.reshape(-1, width) for x in rows]), ffn_w, 1, 0)
        gate, up = both[:, :ffl], both[:, ffl:]
        hidden = (jax.nn.silu(gate) * up).astype(bf16)
        part = dot(hidden, down_w, 1, 0).reshape(len(rows), seqs, slot, width)
        return gate, up, hidden, part

    (near, far), first = window([(own_rows, LINE, 1), (own_rows, LINE, 2)], forward(own_rows))
    (last,), second = window([(far, LINE, 1)], forward(near, far))
    kept = [first, second, forward(last)]
    part = [y for x in kept for y in x[3]]
    normed_mlp = jnp.concatenate([x.reshape(-1, width) for x in (own_rows, near, far, last)])
    hidden = jnp.concatenate([x[2] for x in kept])
    passing = swap(part[3].astype(bf16), LINE, 1)
    got, _ = window(rest_moves([x.astype(bf16) for x in part], passing))
    full = valid * (residual + plus(part[0], got))
    diff = full - teacher.astype(f32)
    (loss,) = tie(jnp.full((1, 64, 128), jnp.sum(valid * diff * diff)))
    loss = lax.all_gather(loss, AXES, axis=0, tiled=True)

    grad_res = valid * (cotangent.astype(f32) + 2.0 * valid * diff / (width * count))
    own_rows = grad_res.astype(bf16)

    def backward(rows, gate, up):
        grad_hidden = dot(jnp.concatenate([x.reshape(-1, width) for x in rows]), down_w, 1, 1)
        sigma = jax.nn.sigmoid(gate)
        slope = sigma * (1.0 + gate * (1.0 - sigma))
        grad_gate = (grad_hidden * up * slope).astype(bf16)
        grad_up = (grad_hidden * gate * sigma).astype(bf16)
        grad_both = jnp.concatenate([grad_gate, grad_up], axis=1)
        return grad_both, dot(grad_both, ffn_w, 1, 1).reshape(len(rows), seqs, slot, width)

    def norm_back(grad_norm, values, scale_rows, gain):
        unit = values * scale_rows
        e = grad_norm * gain
        return scale_rows * (e - unit * jnp.mean(e * unit, axis=-1, keepdims=True))

    (near, far), first = window(
        [(own_rows, LINE, 1), (own_rows, LINE, 2)], backward((own_rows,), *kept[0][:2])
    )
    (last,), second = window([(far, LINE, 1)], backward((near, far), *kept[1][:2]))
    back = [first, second, backward((last,), *kept[2][:2])]
    part = [y for x in back for y in x[1]]
    passing = swap(part[3].astype(bf16), LINE, 1)
    grad_both = jnp.concatenate([x[0] for x in back])
    grad_ffn = jnp.concatenate([x.reshape(-1, width) for x in (own_rows, near, far, last)])
    part, grad_both, hidden = tie(part, grad_both, hidden)
    grad_down = dot(hidden, grad_ffn, 0, 0).astype(bf16).reshape(nb, -1, width)
    passing, grad_down, normed_mlp = tie(passing, grad_down, normed_mlp)
    grad_down = summed(grad_down)
    grad_ffn_w = dot(normed_mlp, grad_both, 0, 0).astype(bf16)
    grad_ffn_w = grad_ffn_w.reshape(nh, 4, cores, drow, -1).transpose(0, 2, 1, 3, 4)
    shares = grad_ffn_w.reshape(nb, 4 * drow, -1)
    got, (shares, loss) = window(rest_moves([x.astype(bf16) for x in part], passing), (shares, loss))
    grad_ffn_w = summed(shares)
    loss = jnp.sum(loss[:, 0, 0]) / (width * count)
    grad_resid = grad_res + norm_back(plus(part[0], got), residual, scale_two, gain_mlp)
    own_rows = grad_resid.astype(bf16)
    got, _ = window(over(own_rows, HEAD))
    sent, grad_out_w = call(
        functools.partial(mixed_back_kernel, hd, copies),
        ids,
        [own_rows] + got + [out_w, mixed],
        [piece(vw), jax.ShapeDtypeStruct((cores, 4, drow, width), bf16)],
        held(vw),
        room=36,
    )
    sent, out_got, _ = exchange(
        sent, far_moves=[(grad_out_w[k], "c", k) for k in range(1, cores)]
    )
    grad_out_w = plus(grad_out_w[0], out_got).astype(bf16)
    sent, grad_out_w = tie(sent, grad_out_w)
    *out_got, out_last = [swap(grad_out_w[o], LINE, o) for o in range(1, 4)]
    grads_out = call(
        functools.partial(bwd_kernel, *geometry),
        ids,
        [tiles, res] + sent,
        piece(pw),
        [
            pltpu.VMEM((n, vw, sb), bf16),
            pltpu.VMEM((n, sb, fw), bf16),
            pltpu.VMEM((n, pw, sb), f32),
        ],
        room=36,
    )
    grads_out, out_got = tie(grads_out, out_got)
    grad_qkv, _, (grad_ffn_w, out_last) = exchange(grads_out, far_beside=(grad_ffn_w, out_last))
    grad_qkv_w, own_back, attn_back = call(
        functools.partial(qkv_back_kernel, hd, copies, fw, vw),
        ids,
        grad_qkv + attn_rows + [qkv_w],
        [jax.ShapeDtypeStruct((cores, 4, nh, drow, hd * pw), bf16), own_part, sent_part],
        taken(pw) + [pltpu.VMEM((hd * pw, seqs * lanes), bf16)],
        room=36,
    )
    grad_qkv_w, grad_ffn_w = tie(grad_qkv_w, grad_ffn_w)
    grad_ffn_w = grad_ffn_w.reshape(4, drow, -1)
    ffn_pieces = [pick(grad_ffn_w, lax.axis_index(LINE) ^ o) for o in range(4)]
    row_moves = [(attn_back[o - 1], HEAD, o) for o in range(1, 4)]
    got, _ = window([(grad_qkv_w[k], "c", k) for k in range(1, cores)])
    grad_qkv_w = plus(grad_qkv_w[0], got).astype(bf16)
    (passing, ffn_2, *row_got), _ = window(
        [by_way(grad_qkv_w), (ffn_pieces[2], LINE, 2)] + row_moves[:2]
    )
    out_got = out_got + [out_last]
    (got_1, got_2, last), _ = window(rest_moves(grad_qkv_w, passing) + [row_moves[2]])
    row_got = row_got + [last]
    grad_qkv_w = plus(grad_qkv_w[0], [got_1, got_2]).astype(bf16)
    (*got, ffn_1, ffn_3), _ = window(
        turn_moves(grad_qkv_w, HEAD) + [(ffn_pieces[1], LINE, 1), (ffn_pieces[3], LINE, 3)]
    )
    rows_f32 = lambda w: jax.ShapeDtypeStruct(w.shape, f32)
    one = jax.ShapeDtypeStruct((drow, 1), f32)
    gg, gu, gain_sum_two = call(
        functools.partial(feed_kernel, nh, run),
        ids,
        [ffn_pieces[0], ffn_1, ffn_2, ffn_3, w_gate, w_up],
        [rows_f32(w_gate), rows_f32(w_up), one],
        [pltpu.VMEM((4, drow, 2 * ffl), bf16)],
    )
    gq, gk, gv, gain_sum_one = call(
        functools.partial(heads_kernel, nh, hd * fw, hd * vw),
        ids,
        [pick(grad_qkv_w, h)] + got + [w_query, w_key, w_value],
        [rows_f32(w_query), rows_f32(w_key), rows_f32(w_value), one],
        [pltpu.VMEM((4, drow, hd * pw), bf16)],
    )
    grad_down, gq, gg = tie(grad_down, gq, gg)
    grad_out_w = plus(grad_out_w[0], out_got)
    grad_in = plus(own_back, row_got)
    grad_tokens = grad_resid + norm_back(grad_in, tokens_f, scale_one, gain_attn)

    def gain_grad(total, gain):
        at = lax.axis_index(AXES) * drow
        return total[:, 0] / lax.dynamic_slice(gain, (at,), (drow,))

    return (
        full.astype(bf16),
        loss,
        grad_tokens,
        gq,
        gk,
        gv,
        grad_out_w.astype(f32),
        gg,
        gu,
        grad_down.astype(f32),
        gain_grad(gain_sum_one, gain_attn),
        gain_grad(gain_sum_two, gain_mlp),
    )


def solution(mesh):
    parts = Mesh(mesh.devices.reshape(mesh.shape["head"], 4, -1), AXES)
    rows, slots = P(AXES, None), P(None, AXES, None)
    return jax.shard_map(
        shards,
        mesh=parts,
        in_specs=(slots,) * 3 + (P(),) * 3 + (rows,) * 7,
        out_specs=(slots, P(), slots) + (rows,) * 7 + (P(AXES),) * 2,
        check_vma=False,
    )
```

```python
import functools
import math

import jax
import jax.numpy as jnp
from jax import lax
from jax.experimental import pallas as pl
from jax.experimental.pallas import tpu as pltpu
from jax.sharding import Mesh
from jax.sharding import PartitionSpec as P

H = 16
norm_eps = 1e-06
bf16, f32 = jnp.bfloat16, jnp.float32


def dot(a, b, ca, cb):
    return lax.dot_general(a, b, (((ca,), (cb,)), ((), ())), preferred_element_type=f32)


def swap(x, axis, o):
    n = lax.axis_size(axis)
    return lax.ppermute(x, axis, [(i, i ^ o) for i in range(n)])


def rms_scale(values):
    return lax.rsqrt(jnp.mean(values * values, axis=-1, keepdims=True) + norm_eps)


HEAD, LINE, BLK, CROSS = "head", "z", ("z", "c"), ("head", "c")
AXES = (HEAD,) + BLK


def tie(*values):
    return lax.optimization_barrier(values)


def window(moves, beside=()):
    arrays = tie(*[x for x, _, _ in moves])
    return tie([swap(x, axis, o) for x, (_, axis, o) in zip(arrays, moves)], beside)


def over(x, axis):
    return [(x, axis, o) for o in range(1, lax.axis_size(axis))]


def turn_moves(pieces, axis):
    me = lax.axis_index(axis)
    return [(pick(pieces, me ^ o), axis, o) for o in range(1, lax.axis_size(axis))]


def turned(pieces, got, axis):
    me = lax.axis_index(axis)
    return in_place([pick(pieces, me)] + list(got), me)


def return_moves(parts, axis):
    return [(x, axis, o) for o, x in enumerate(parts) if o]


def plus(own, got):
    return sum([x.astype(f32) for x in got], own.astype(f32))


def by_way(blocks):
    return (blocks[3], LINE, 1)


def rest_moves(blocks, passing):
    far = (blocks[2].astype(f32) + passing.astype(f32)).astype(bf16)
    return [(blocks[1], LINE, 1), (far, LINE, 2)]


def exchange(pieces, far_moves=(), far_beside=(), near_beside=()):
    got, near_beside = window([(pieces[k], "c", k) for k in range(1, pieces.shape[0])], near_beside)
    near = jnp.stack([pieces[0]] + got, axis=1)
    far_moves = far_moves(*near_beside) if callable(far_moves) else far_moves
    got, far_beside = window([(near[o], LINE, o) for o in range(1, 4)] + list(far_moves), far_beside)
    return [near[0]] + got[:3], got[3:], far_beside + near_beside


def in_place(got, me):
    whole = jnp.zeros((len(got),) + got[0].shape, got[0].dtype)
    for o, x in enumerate(got):
        whole = lax.dynamic_update_index_in_dim(whole, x, me ^ o, 0)
    return whole


def pick(x, i, axis=0):
    return lax.dynamic_index_in_dim(x, i, axis, keepdims=False)


def line_whole(got):
    return in_place(got, lax.axis_index(LINE))


def core_end(own, got):
    return jnp.moveaxis(in_place([own] + list(got), lax.axis_index("c")), 0, 1)


def core_share(parts, at):
    me = lax.axis_index("c")
    return [(pick(parts, me ^ o, at), "c", o) for o in range(1, lax.axis_size("c"))]


def core_sum(parts, got, at):
    return plus(pick(parts, lax.axis_index("c"), at), got).astype(bf16)


def line_blocks(near, at):
    return [pick(near, lax.axis_index(LINE) ^ o, at) for o in range(4)]


def positions(b, sub, cps, slot, dim, sb):
    shape = (sb, 1) if dim == 0 else (1, sb)
    lane = lax.broadcasted_iota(jnp.int32, shape, dim)
    return ((b ^ (sub * cps + lane // slot)) * slot) + lane % slot


def flip(x, factor=1.0):
    return jnp.transpose(x.astype(f32) * factor).astype(bf16)


def lifted(qrow, kcol):
    return dot(qrow, kcol, 1, 0) + 1.0


def repeat(lo, hi, step, value):
    if hi - lo <= 4:
        for i in range(lo, hi):
            value = step(i, value)
        return value
    return lax.fori_loop(lo, hi, step, value)


def fwd_kernel(nh, nb, slot, sb, ids, got0, got1, got2, got3, tiles, res, out, vrow, back):
    got, cores = (got0, got1, got2, got3), nb // 4
    nsub, cps = nb * slot // sb, sb // slot
    h, b = ids[0], ids[1]
    for o in range(nb):
        for oh in range(nh):
            at = (h ^ oh) * nsub + o // cps
            lo = (o % cps) * slot
            piece = got[o // cores][o % cores, :, oh * slot : (oh + 1) * slot]
            tiles[at, :, lo : lo + slot] = piece

    def rows_of(i, c):
        vv = jnp.concatenate([tiles[i, 32:144, :].astype(f32), jnp.ones((16, sb), f32)], axis=0)
        vrow[i] = jnp.transpose(vv).astype(bf16)
        return c

    repeat(0, nh * nsub, rows_of, 0)

    for hq in range(nh):
        for sub in range(nsub):
            iq = hq * nsub + sub
            qrow = flip(tiles[iq, 0:16, :], 0.25)
            pos_q = positions(b, sub, cps, slot, 0, sb)

            def step(ik, acc, masked):
                u = lifted(qrow, tiles[ik, 16:32, :])
                w = u * u + 1.0
                if masked:
                    pos_k = positions(b, ik - hq * nsub, cps, slot, 1, sb)
                    w = jnp.where(pos_q >= pos_k, w, 0.0)
                return acc + dot(w.astype(bf16), vrow[ik], 1, 0)

            acc = jnp.zeros((sb, 128), f32)
            acc = repeat(0, hq * nsub, functools.partial(step, masked=False), acc)
            acc = repeat(hq * nsub, (hq + 1) * nsub, functools.partial(step, masked=True), acc)
            den = acc[:, 112:113]
            mixed = acc / den
            lane = lax.broadcasted_iota(jnp.int32, (sb, 128), 1)
            res[iq] = jnp.where(lane == 112, den, mixed)
            back[iq] = jnp.transpose(mixed)[0:112].astype(bf16)
    for oh in range(nh):
        for o in range(nb):
            lo = (o % cps) * slot
            piece = back[(h ^ oh) * nsub + o // cps, :, lo : lo + slot]
            out[o % cores, o // cores, :, oh * slot : (oh + 1) * slot] = piece


def bwd_kernel(nh, nb, slot, sb, ids, tiles, res, got0, got1, got2, got3, out, gt, krow, acc):
    got, cores = (got0, got1, got2, got3), nb // 4
    nsub, cps = nb * slot // sb, sb // slot
    h, b = ids[0], ids[1]
    for o in range(nb):
        for oh in range(nh):
            at = (h ^ oh) * nsub + o // cps
            lo = (o % cps) * slot
            piece = got[o // cores][o % cores, :, oh * slot : (oh + 1) * slot]
            gt[at, :, lo : lo + slot] = piece

    def rows_of(i, c):
        krow[i] = flip(tiles[i, 16:32, :])
        acc[i] = jnp.zeros((144, sb), f32)
        return c

    repeat(0, nh * nsub, rows_of, 0)

    for hq in range(nh):
        for sub in range(nsub):
            iq = hq * nsub + sub
            qcol = tiles[iq, 0:16, :]
            qrow = flip(qcol, 0.25)
            gcol = gt[iq]
            grow = jnp.transpose(gcol.astype(f32))
            kept = res[iq]
            rden = 1.0 / kept[:, 112:113]
            rquarter = rden * 0.5
            delta = jnp.sum(grow * kept[:, 0:112], axis=1, keepdims=True)
            grow = grow.astype(bf16)
            pos_q = positions(b, sub, cps, slot, 0, sb)

            def step(ik, dq, masked):
                u = lifted(qrow, tiles[ik, 16:32, :])
                p = (u * u + 1.0) * rden
                ds = (dot(grow, tiles[ik, 32:144, :], 1, 0) - delta) * rquarter * u
                if masked:
                    pos_k = positions(b, ik - hq * nsub, cps, slot, 1, sb)
                    keep = pos_q >= pos_k
                    p = jnp.where(keep, p, 0.0)
                    ds = jnp.where(keep, ds, 0.0)
                p, ds = p.astype(bf16), ds.astype(bf16)
                acc[ik, 32:144, :] += dot(gcol, p, 1, 0)
                acc[ik, 16:32, :] += dot(qcol, ds, 1, 0)
                return dq + dot(ds, krow[ik], 1, 0)

            dq = jnp.zeros((sb, 16), f32)
            dq = repeat(0, hq * nsub, functools.partial(step, masked=False), dq)
            dq = repeat(hq * nsub, (hq + 1) * nsub, functools.partial(step, masked=True), dq)
            acc[iq, 0:16, :] = jnp.transpose(dq)
    for oh in range(nh):
        for o in range(nb):
            at = (h ^ oh) * nsub + o // cps
            lo = (o % cps) * slot
            piece = acc[at, :, lo : lo + slot].astype(bf16)
            out[o % cores, o // cores, :, oh * slot : (oh + 1) * slot] = piece


def rows_of(refs, s):
    return jnp.concatenate([x[s] for x in refs], axis=0)


def to_peers(cores, copies, b, pieces, out):
    for o in range(4 * cores):
        out[o % cores, o // cores] = pieces[(b ^ o) // copies]


def from_peers(cores, copies, b, got, pieces):
    for o in range(4 * cores):
        pieces[o] = got[o // cores][o % cores]
    return lambda p: pieces[b ^ (p * copies)]


def qkv_kernel(hd, copies, fw, vw, ids, x0, x1, x2, x3, w, out, pieces):
    cores = out.shape[0]
    for s in range(x0.shape[0]):
        rows = jnp.dot(rows_of((x0, x1, x2, x3), s), w[...], preferred_element_type=f32)
        cols = jnp.transpose(rows)
        for j in range(hd):
            at = (j * fw, (hd + j) * fw, 2 * hd * fw + j * vw)
            piece = [cols[lo : lo + n] for lo, n in zip(at, (fw, fw, vw))]
            pieces[s * hd + j] = jnp.concatenate(piece, axis=0).astype(bf16)
    to_peers(cores, copies, ids[1], pieces, out)


def out_kernel(hd, copies, ids, g0, g1, g2, g3, w, mixed, own, send, pieces):
    cores, vw, lanes = g0.shape
    seqs, slot = own.shape[:2]
    take = from_peers(cores, copies, ids[1], (g0, g1, g2, g3), pieces)
    for s in range(seqs):
        cols = jnp.concatenate([take(s * hd + j) for j in range(hd)], axis=0)
        mixed[:, s * lanes : (s + 1) * lanes] = cols
        rows = jnp.transpose(cols.astype(f32)).astype(bf16)
        part = jnp.dot(rows, w[...], preferred_element_type=f32)
        own[s] = part[:slot]
        for o in range(1, 4):
            send[o - 1, s] = part[o * slot : (o + 1) * slot].astype(bf16)


def mixed_back_kernel(hd, copies, ids, x0, x1, x2, x3, w, mixed, out, grad, pieces):
    cores, vw, lanes = out.shape[0], out.shape[2], out.shape[3]
    z, c = ids[2], ids[1] % cores
    rows = [rows_of((x0, x1, x2, x3), s) for s in range(x0.shape[0])]
    for s, x in enumerate(rows):
        cols = dot(w[...], x, 1, 1)
        for j in range(hd):
            pieces[s * hd + j] = cols[j * vw : (j + 1) * vw].astype(bf16)
    to_peers(cores, copies, ids[1], pieces, out)
    total = jnp.dot(mixed[...], jnp.concatenate(rows, axis=0), preferred_element_type=f32)
    drow = grad.shape[2]
    for k in range(4 * cores):
        grad[(k % cores) ^ c, (k // cores) ^ z] = total[k * drow : (k + 1) * drow].astype(bf16)


def qkv_back_kernel(
    hd, copies, fw, vw, ids, g0, g1, g2, g3, x0, x1, x2, x3, w, grad, own, send, pieces, cols
):
    cores, pw, lanes = g0.shape
    seqs, slot = own.shape[:2]
    z, c = ids[2], ids[1] % cores
    take = from_peers(cores, copies, ids[1], (g0, g1, g2, g3), pieces)
    for s in range(seqs):
        for j in range(hd):
            piece = take(s * hd + j)
            at = (j * fw, (hd + j) * fw, 2 * hd * fw + j * vw)
            lo = 0
            for row, n in zip(at, (fw, fw, vw)):
                cols[row : row + n, s * lanes : (s + 1) * lanes] = piece[lo : lo + n]
                lo += n
    rows = jnp.transpose(cols[...].astype(f32)).astype(bf16)
    for s in range(seqs):
        part = dot(rows[s * lanes : (s + 1) * lanes], w[...], 1, 1)
        own[s] = part[:slot]
        for o in range(1, 4):
            send[o - 1, s] = part[o * slot : (o + 1) * slot].astype(bf16)
    x = jnp.concatenate([rows_of((x0, x1, x2, x3), s) for s in range(seqs)], axis=0)
    drow, half = grad.shape[3], x.shape[1] // 2
    for i in range(2):
        total = dot(x[:, i * half : (i + 1) * half], rows, 0, 0)
        for k in range(half // drow):
            at = i * (half // drow) + k
            block = total[k * drow : (k + 1) * drow].astype(bf16)
            grad[(at % cores) ^ c, (at // cores % 4) ^ z, at // (4 * cores)] = block


def ffn_back_kernel(cores, ids, x, g, out):
    heads, drow = out.shape[0], out.shape[3]
    total = dot(x[...], g[...], 0, 0)
    for k in range(heads * 4 * cores):
        block = total[k * drow : (k + 1) * drow].astype(bf16)
        out[k // (4 * cores), k % cores, k // cores % 4] = block


def cut_kernel(nh, run, ids, gate, up, wq, wk, wv, out, heads):
    h, z = ids[0], ids[2]
    qw, vw = wq.shape[1] // nh, wv.shape[1] // nh
    for k in range(nh):
        parts = [wq[:, k * qw : (k + 1) * qw], wk[:, k * qw : (k + 1) * qw]]
        parts.append(wv[:, k * vw : (k + 1) * vw])
        heads[k ^ h] = jnp.concatenate([x.astype(f32) for x in parts], axis=1).astype(bf16)
    for zz in range(4):
        parts = []
        for w in (gate, up):
            parts += [w[:, (k * 4 + zz) * run : (k * 4 + zz + 1) * run] for k in range(nh)]
        out[zz ^ z] = jnp.concatenate([x.astype(f32) for x in parts], axis=1).astype(bf16)


def feed_kernel(nh, run, ids, p0, p1, p2, p3, gate, up, grad_gate, grad_up, total, pieces):
    z = ids[2]
    pieces[0], pieces[1], pieces[2], pieces[3] = p0[...], p1[...], p2[...], p3[...]
    for zz in range(4):
        piece = pieces[zz ^ z].astype(f32)
        for at, grad in ((0, grad_gate), (nh * run, grad_up)):
            for k in range(nh):
                lo = (k * 4 + zz) * run
                grad[:, lo : lo + run] = piece[:, at + k * run : at + (k + 1) * run]
    both = grad_gate[...] * gate[...].astype(f32) + grad_up[...] * up[...].astype(f32)
    total[...] = jnp.sum(both, axis=1, keepdims=True)


def heads_kernel(nh, qw, vw, ids, p0, p1, p2, p3, wq, wk, wv, gq, gk, gv, total, pieces):
    h = ids[0]
    pieces[0], pieces[1], pieces[2], pieces[3] = p0[...], p1[...], p2[...], p3[...]
    for k in range(nh):
        piece = pieces[k ^ h].astype(f32)
        gq[:, k * qw : (k + 1) * qw] = piece[:, :qw]
        gk[:, k * qw : (k + 1) * qw] = piece[:, qw : 2 * qw]
        gv[:, k * vw : (k + 1) * vw] = piece[:, 2 * qw :]
    sums = [
        jnp.sum(g[...] * w[...].astype(f32), axis=1, keepdims=True)
        for g, w in ((gq, wq), (gk, wk), (gv, wv))
    ]
    total[...] = sums[0] + sums[1] + sums[2]


def call(body, ids, arrays, outs, scratch, room=12):
    vmem = pl.BlockSpec(memory_space=pltpu.VMEM)
    held = list(arrays) + jax.tree.leaves(outs) + list(scratch)
    held = sum(math.prod(x.shape[:-1]) * max(x.shape[-1], 128) * x.dtype.itemsize for x in held)
    return pl.pallas_call(
        body,
        out_shape=outs,
        in_specs=[pl.BlockSpec(memory_space=pltpu.SMEM)] + [vmem] * len(arrays),
        out_specs=jax.tree.map(lambda _: vmem, outs),
        scratch_shapes=scratch,
        compiler_params=pltpu.CompilerParams(vmem_limit_bytes=held + room * 1024 * 1024),
    )(ids, *arrays)


def shards(
    tokens,
    cotangent,
    teacher,
    lengths,
    gain_attn,
    gain_mlp,
    w_query,
    w_key,
    w_value,
    w_out,
    w_gate,
    w_up,
    w_down,
):
    seqs, slot, width = tokens.shape
    cores = lax.axis_size("c")
    nh, nb = lax.axis_size(HEAD), 4 * cores
    h, b = lax.axis_index(HEAD), lax.axis_index(BLK)
    hd = H // nh
    pairs = seqs * hd
    copies = nb // pairs
    drow = w_query.shape[0]
    fw, vw = w_query.shape[1] // H, w_value.shape[1] // H
    pw = 2 * fw + vw
    ffl = w_gate.shape[1] // 4
    lanes = nh * slot
    sb = min(512, nb * slot)
    n = nb * slot * nh // sb
    ids = jnp.stack([h, b, lax.axis_index(LINE)]).astype(jnp.int32)

    def gathered(x):
        return lax.all_gather(x[None], CROSS, axis=0, tiled=True)

    def summed(shares):
        return lax.psum_scatter(shares, CROSS, scatter_dimension=0)

    run = w_gate.shape[1] // (4 * nh)
    ffn_cols, qkv_cols = call(
        functools.partial(cut_kernel, nh, run),
        ids,
        [w_gate, w_up, w_query, w_key, w_value],
        [
            jax.ShapeDtypeStruct((4, drow, 2 * ffl), bf16),
            jax.ShapeDtypeStruct((nh, drow, hd * pw), bf16),
        ],
        [],
    )

    place = (h * nb + b) * slot + lax.broadcasted_iota(jnp.int32, (seqs, slot), 1)
    valid = (place < lengths[:, None]).astype(f32)[..., None]
    count = jnp.sum(lengths).astype(f32)

    tokens_f = tokens.astype(f32)
    scale_one = rms_scale(tokens_f)
    own_rows = (tokens_f * scale_one * gain_attn).astype(bf16)
    (*got, ffn_1, ffn_2), (own_rows,) = window(
        return_moves(qkv_cols, HEAD) + [(ffn_cols[1], LINE, 1), (ffn_cols[2], LINE, 2)], (own_rows,)
    )
    qkv_cols = in_place([qkv_cols[0]] + got, h)
    (row_1, row_2, qkv_near, qkv_far), _ = window(
        [(own_rows, HEAD, 1), (own_rows, HEAD, 2), (qkv_cols, LINE, 1), (qkv_cols, LINE, 2)]
    )
    (row_3, qkv_last, ffn_3), _ = window(
        [(own_rows, HEAD, 3), (qkv_far, LINE, 1), (ffn_cols[3], LINE, 3)]
    )
    attn_rows = [own_rows, row_1, row_2, row_3]
    qkv_w = line_whole([qkv_cols, qkv_near, qkv_far, qkv_last])
    got, (ffn_cols,) = window(
        over(qkv_w, "c"), (line_whole([ffn_cols[0], ffn_1, ffn_2, ffn_3]),)
    )
    ffn_w = gathered(ffn_cols)
    ffn_w = ffn_w.reshape(nh, cores, 4, drow, -1).transpose(0, 2, 1, 3, 4).reshape(width, -1)
    qkv_w = core_end(qkv_w, got).transpose(2, 0, 1, 3, 4).reshape(width, -1)
    geometry = (nh, nb, slot, sb)
    piece = lambda rows: jax.ShapeDtypeStruct((cores, 4, rows, lanes), bf16)
    held = lambda rows: [pltpu.VMEM((pairs, rows, lanes), bf16)]
    taken = lambda rows: [pltpu.VMEM((nb, rows, lanes), bf16)]
    own_part = jax.ShapeDtypeStruct((seqs, slot, width), f32)
    sent_part = jax.ShapeDtypeStruct((3, seqs, slot, width), bf16)
    pieces = call(
        functools.partial(qkv_kernel, hd, copies, fw, vw),
        ids,
        attn_rows + [qkv_w],
        piece(pw),
        held(pw),
        room=36,
    )
    sent, _, (down_w, w_out_late) = exchange(pieces, far_beside=(gathered(w_down), w_out))
    down_w = down_w.reshape(-1, width)
    out_near, out_far = swap(w_out_late, LINE, 1), swap(w_out_late, LINE, 2)
    tiles, res, mixed_out = call(
        functools.partial(fwd_kernel, *geometry),
        ids,
        sent,
        [
            jax.ShapeDtypeStruct((n, pw, sb), bf16),
            jax.ShapeDtypeStruct((n, sb, 128), f32),
            piece(vw),
        ],
        [pltpu.VMEM((n, sb, 128), bf16), pltpu.VMEM((n, vw, sb), bf16)],
        room=36,
    )
    mixed_got, (out_last,), (out_near, out_far) = exchange(
        mixed_out,
        far_moves=lambda near, far: [(far, LINE, 1)],
        near_beside=(out_near, out_far),
    )
    out_w = line_whole([w_out, out_near, out_far, out_last])
    got, (out_w,) = window(over(out_w, "c"), (out_w,))
    out_w = core_end(out_w, got).reshape(-1, width)
    mixed, attn_own, attn_part = call(
        functools.partial(out_kernel, hd, copies),
        ids,
        mixed_got + [out_w],
        [jax.ShapeDtypeStruct((hd * vw, seqs * lanes), bf16), own_part, sent_part],
        taken(vw),
        room=36,
    )
    got, (ffn_w,) = window([(attn_part[o - 1], HEAD, o) for o in range(1, 4)], (ffn_w,))
    residual = tokens_f + plus(attn_own, got)

    scale_two = rms_scale(residual)
    own_rows = (residual * scale_two * gain_mlp).astype(bf16)

    def forward(*rows):
        both = dot(jnp.concatenate([x.reshape(-1, width) for x in rows]), ffn_w, 1, 0)
        gate, up = both[:, :ffl], both[:, ffl:]
        hidden = (jax.nn.silu(gate) * up).astype(bf16)
        part = dot(hidden, down_w, 1, 0).reshape(len(rows), seqs, slot, width)
        return gate, up, hidden, part

    (near, far), first = window([(own_rows, LINE, 1), (own_rows, LINE, 2)], forward(own_rows))
    (last,), second = window([(far, LINE, 1)], forward(near, far))
    kept = [first, second, forward(last)]
    part = [y for x in kept for y in x[3]]
    normed_mlp = jnp.concatenate([x.reshape(-1, width) for x in (own_rows, near, far, last)])
    hidden = jnp.concatenate([x[2] for x in kept])
    passing = swap(part[3].astype(bf16), LINE, 1)
    got, _ = window(rest_moves([x.astype(bf16) for x in part], passing))
    full = valid * (residual + plus(part[0], got))
    diff = full - teacher.astype(f32)
    (loss,) = tie(jnp.full((1, 64, 128), jnp.sum(valid * diff * diff)))
    loss = lax.all_gather(loss, AXES, axis=0, tiled=True)

    grad_res = valid * (cotangent.astype(f32) + 2.0 * valid * diff / (width * count))
    own_rows = grad_res.astype(bf16)

    def backward(rows, gate, up):
        grad_hidden = dot(jnp.concatenate([x.reshape(-1, width) for x in rows]), down_w, 1, 1)
        sigma = jax.nn.sigmoid(gate)
        slope = sigma * (1.0 + gate * (1.0 - sigma))
        grad_gate = (grad_hidden * up * slope).astype(bf16)
        grad_up = (grad_hidden * gate * sigma).astype(bf16)
        grad_both = jnp.concatenate([grad_gate, grad_up], axis=1)
        return grad_both, dot(grad_both, ffn_w, 1, 1).reshape(len(rows), seqs, slot, width)

    def norm_back(grad_norm, values, scale_rows, gain):
        unit = values * scale_rows
        e = grad_norm * gain
        return scale_rows * (e - unit * jnp.mean(e * unit, axis=-1, keepdims=True))

    (near, far), first = window(
        [(own_rows, LINE, 1), (own_rows, LINE, 2)], backward((own_rows,), *kept[0][:2])
    )
    (last,), second = window([(far, LINE, 1)], backward((near, far), *kept[1][:2]))
    back = [first, second, backward((last,), *kept[2][:2])]
    part = [y for x in back for y in x[1]]
    passing = swap(part[3].astype(bf16), LINE, 1)
    grad_both = jnp.concatenate([x[0] for x in back])
    grad_ffn = jnp.concatenate([x.reshape(-1, width) for x in (own_rows, near, far, last)])
    part, grad_both, hidden = tie(part, grad_both, hidden)
    grad_down = dot(hidden, grad_ffn, 0, 0).astype(bf16).reshape(nb, -1, width)
    passing, grad_down, normed_mlp = tie(passing, grad_down, normed_mlp)
    grad_down = summed(grad_down)
    rows, cols = normed_mlp.shape[0], grad_both.shape[1]
    shares = pl.pallas_call(
        functools.partial(ffn_back_kernel, cores),
        grid=(2,),
        out_shape=jax.ShapeDtypeStruct((nh, cores, 4, drow, cols), bf16),
        in_specs=[
            pl.BlockSpec(memory_space=pltpu.SMEM),
            pl.BlockSpec((rows, width // 2), lambda i: (0, i)),
            pl.BlockSpec((rows, cols), lambda i: (0, 0)),
        ],
        out_specs=pl.BlockSpec((nh // 2, cores, 4, drow, cols), lambda i: (i, 0, 0, 0, 0)),
        compiler_params=pltpu.CompilerParams(vmem_limit_bytes=40 * 1024 * 1024),
    )(ids, normed_mlp, grad_both)
    shares = shares.reshape(nh * cores, 4 * drow, -1)
    got, (shares, loss) = window(rest_moves([x.astype(bf16) for x in part], passing), (shares, loss))
    grad_ffn_w = summed(shares)
    loss = jnp.sum(loss[:, 0, 0]) / (width * count)
    grad_resid = grad_res + norm_back(plus(part[0], got), residual, scale_two, gain_mlp)
    own_rows = grad_resid.astype(bf16)
    got, _ = window(over(own_rows, HEAD))
    sent, grad_out_w = call(
        functools.partial(mixed_back_kernel, hd, copies),
        ids,
        [own_rows] + got + [out_w, mixed],
        [piece(vw), jax.ShapeDtypeStruct((cores, 4, drow, width), bf16)],
        held(vw),
        room=36,
    )
    sent, out_got, _ = exchange(
        sent, far_moves=[(grad_out_w[k], "c", k) for k in range(1, cores)]
    )
    grad_out_w = plus(grad_out_w[0], out_got).astype(bf16)
    sent, grad_out_w = tie(sent, grad_out_w)
    *out_got, out_last = [swap(grad_out_w[o], LINE, o) for o in range(1, 4)]
    grads_out = call(
        functools.partial(bwd_kernel, *geometry),
        ids,
        [tiles, res] + sent,
        piece(pw),
        [
            pltpu.VMEM((n, vw, sb), bf16),
            pltpu.VMEM((n, sb, fw), bf16),
            pltpu.VMEM((n, pw, sb), f32),
        ],
        room=36,
    )
    grads_out, out_got = tie(grads_out, out_got)
    grad_qkv, _, (grad_ffn_w, out_last) = exchange(grads_out, far_beside=(grad_ffn_w, out_last))
    grad_qkv_w, own_back, attn_back = call(
        functools.partial(qkv_back_kernel, hd, copies, fw, vw),
        ids,
        grad_qkv + attn_rows + [qkv_w],
        [jax.ShapeDtypeStruct((cores, 4, nh, drow, hd * pw), bf16), own_part, sent_part],
        taken(pw) + [pltpu.VMEM((hd * pw, seqs * lanes), bf16)],
        room=36,
    )
    grad_qkv_w, grad_ffn_w = tie(grad_qkv_w, grad_ffn_w)
    grad_ffn_w = grad_ffn_w.reshape(4, drow, -1)
    ffn_pieces = [pick(grad_ffn_w, lax.axis_index(LINE) ^ o) for o in range(4)]
    row_moves = [(attn_back[o - 1], HEAD, o) for o in range(1, 4)]
    got, _ = window([(grad_qkv_w[k], "c", k) for k in range(1, cores)])
    grad_qkv_w = plus(grad_qkv_w[0], got).astype(bf16)
    (passing, ffn_2, *row_got), _ = window(
        [by_way(grad_qkv_w), (ffn_pieces[2], LINE, 2)] + row_moves[:2]
    )
    out_got = out_got + [out_last]
    (got_1, got_2, last), _ = window(rest_moves(grad_qkv_w, passing) + [row_moves[2]])
    row_got = row_got + [last]
    grad_qkv_w = plus(grad_qkv_w[0], [got_1, got_2]).astype(bf16)
    (*got, ffn_1, ffn_3), _ = window(
        turn_moves(grad_qkv_w, HEAD) + [(ffn_pieces[1], LINE, 1), (ffn_pieces[3], LINE, 3)]
    )
    rows_f32 = lambda w: jax.ShapeDtypeStruct(w.shape, f32)
    one = jax.ShapeDtypeStruct((drow, 1), f32)
    gg, gu, gain_sum_two = call(
        functools.partial(feed_kernel, nh, run),
        ids,
        [ffn_pieces[0], ffn_1, ffn_2, ffn_3, w_gate, w_up],
        [rows_f32(w_gate), rows_f32(w_up), one],
        [pltpu.VMEM((4, drow, 2 * ffl), bf16)],
    )
    gq, gk, gv, gain_sum_one = call(
        functools.partial(heads_kernel, nh, hd * fw, hd * vw),
        ids,
        [pick(grad_qkv_w, h)] + got + [w_query, w_key, w_value],
        [rows_f32(w_query), rows_f32(w_key), rows_f32(w_value), one],
        [pltpu.VMEM((4, drow, hd * pw), bf16)],
    )
    grad_down, gq, gg = tie(grad_down, gq, gg)
    grad_out_w = plus(grad_out_w[0], out_got)
    grad_in = plus(own_back, row_got)
    grad_tokens = grad_resid + norm_back(grad_in, tokens_f, scale_one, gain_attn)

    def gain_grad(total, gain):
        at = lax.axis_index(AXES) * drow
        return total[:, 0] / lax.dynamic_slice(gain, (at,), (drow,))

    return (
        full.astype(bf16),
        loss,
        grad_tokens,
        gq,
        gk,
        gv,
        grad_out_w.astype(f32),
        gg,
        gu,
        grad_down.astype(f32),
        gain_grad(gain_sum_one, gain_attn),
        gain_grad(gain_sum_two, gain_mlp),
    )


def solution(mesh):
    parts = Mesh(mesh.devices.reshape(mesh.shape["head"], 4, -1), AXES)
    rows, slots = P(AXES, None), P(None, AXES, None)
    return jax.shard_map(
        shards,
        mesh=parts,
        in_specs=(slots,) * 3 + (P(),) * 3 + (rows,) * 7,
        out_specs=(slots, P(), slots) + (rows,) * 7 + (P(AXES),) * 2,
        check_vma=False,
    )
```
